128 devices in a mesh: dp: 16 (over y, z), ctx: 8 (over x, core).
Axes of the slice: x: 4, y: 4, z: 4, core: 2. Of those that a mesh axis runs over, the one named last changes fastest.
Arguments:
- queries: bfloat16 [16, 1024, 1024], P('dp', 'ctx'), may hold values from -48 to 48
- keys: bfloat16 [16, 1024, 1024], P('dp', 'ctx'), may hold values from -8 to 8
- values: bfloat16 [16, 1024, 1024], P('dp', 'ctx'), may hold values from -6 to 6
- directions: bfloat16 [16, 1024, 1024], P('dp', 'ctx'), may hold values from -6 to 6
- beta_logits: float32 [16, 8, 1024], P('dp', None, 'ctx'), may hold values from -24 to 10
- out_proj: bfloat16 [1024, 4096], replicated, may hold values from -0.1875 to 0.1875
- out_grad: bfloat16 [16, 1024, 4096], P('dp', 'ctx'), may hold values from -6 to 6
- doc_lengths: int32 [16, 4], P('dp'), may hold values from 1 to 640, 1024 in all within a row
Outputs:
- grad_queries: bfloat16 [16, 1024, 1024], P('dp', 'ctx')
- grad_keys: bfloat16 [16, 1024, 1024], P('dp', 'ctx')
- grad_values: bfloat16 [16, 1024, 1024], P('dp', 'ctx')
- grad_directions: bfloat16 [16, 1024, 1024], P('dp', 'ctx')
- grad_beta: float32 [16, 8, 1024], P('dp', None, 'ctx')
- grad_proj: float32 [1024, 4096], P(('dp', 'ctx'))
The draws below stay inside these ranges and needn't reach their ends.
All inputs are finite; a program needn't handle non-finite values.
Results may differ from the reference program's by a relative error of at most 0.015.
Values may be sent and summed in bfloat16 or wider, within the bound.
A program may use at most 128 MiB of HBM per device.

```python
import math
import jax
import jax.numpy as jnp
import numpy as np
from jax import lax

D = 4096
HEADS = 8
DOCS = 4
TOK_DEV = 128
HK = 1024
SEQS = 16
TOKENS = 1024
LONGEST = 640


def draw_keys(key, part):
    key = jax.random.fold_in(key, 2)
    result = jnp.clip(jax.random.normal(key, (SEQS, TOKENS, HK), jnp.float32), -6.0, 6.0)
    return result.astype(jnp.bfloat16)


def draw_queries(key, part):
    key = jax.random.fold_in(key, 3)
    result = jnp.clip(jax.random.normal(key, (SEQS, TOKENS, HK), jnp.float32), -6.0, 6.0)
    return result.astype(jnp.bfloat16)


def draw_beta_logits(key, part):
    key = jax.random.fold_in(key, 4)
    offset = jax.random.uniform(jax.random.fold_in(key, 6), (SEQS, HEADS, 1), jnp.float32, -2.0, 3.0)
    noise = 1.5 * jnp.clip(jax.random.normal(key, (SEQS, HEADS, TOKENS), jnp.float32), -4.0, 4.0)
    result = offset + noise
    return result


def steps_of(own_key, extent, cuts, smallest, largest):
    def one(dim, blocks):
        draws = jax.random.uniform(jax.random.fold_in(jax.random.fold_in(own_key, 6), dim), (blocks,), jnp.float32, smallest / len(cuts), largest / len(cuts))
        return jnp.repeat(jnp.exp(draws), extent[dim] // blocks).reshape((-1,) + (1,) * (len(extent) - dim - 1))

    level = one(*cuts[0])
    for cut in cuts[1:]:
        level = level * one(*cut)
    return level


def split_up(number_of, total, bound, lean):
    weights = [(1 << 20) // math.isqrt(rank ** lean) + 1 for rank in range(2, number_of + 1)]
    surplus, counts = total - bound - (number_of - 1), [1] * (number_of - 1)
    while surplus > 0:
        movable = [i for i in range(number_of - 1) if counts[i] < bound]
        mass, remaining = sum([weights[i] for i in movable]), surplus
        for i in movable:
            extra = min(bound - counts[i], max(1, remaining * weights[i] // mass), surplus)
            counts[i] = counts[i] + extra
            surplus = surplus - extra
    return np.array([bound] + counts)


def ragged(own_key, number_of, total, limit, skew):
    if number_of == 2:
        one = jax.random.randint(own_key, (), max(1, total - limit), min(limit, total - 1) + 1)
        return jnp.stack([one, total - one])
    sizes = jnp.asarray(split_up(number_of, total, limit, skew), jnp.int32)
    couples = (number_of - 1) // 2
    source_of, receiver = sizes[1:1 + 2 * couples:2], sizes[2:2 + 2 * couples:2]
    slack = jnp.minimum(source_of - 1, limit - receiver)
    shifted = jax.random.randint(jax.random.fold_in(own_key, 1), (couples,), 0, 1 << 20) % (slack + 1)
    sizes = sizes.at[1:1 + 2 * couples:2].set(source_of - shifted).at[2:2 + 2 * couples:2].set(receiver + shifted)
    return sizes[jax.random.permutation(jax.random.fold_in(own_key, 2), number_of)]


def scatter_about(key, dims, deviation, reach, cuts=(), kind=jnp.bfloat16):
    loudness = steps_of(key, dims, cuts, -0.22, 0.18) if cuts else 1.0
    values = jax.random.normal(key, dims, jnp.float32) * deviation * loudness
    return jnp.minimum(jnp.maximum(values, -reach), reach).astype(kind)


def setup_inputs(seed: int = 0) -> dict:
    key_list = jax.random.split(jax.random.key(seed), 9)
    queries = draw_queries(jax.random.fold_in(key_list[8], 71), 0)
    keys = draw_keys(jax.random.fold_in(key_list[8], 71), 0)
    values = scatter_about(key_list[2], (SEQS, TOKENS, HK), 1.0, 6.0, ((0, 16), (1, 8)))
    directions = scatter_about(key_list[3], (SEQS, TOKENS, HK), 1.0, 6.0, ((0, 16), (1, 8)))
    beta_logits = draw_beta_logits(jax.random.fold_in(key_list[8], 71), 0)
    out_proj = scatter_about(key_list[5], (HK, D), HK ** -0.5, 0.1875)
    out_grad = scatter_about(key_list[6], (SEQS, TOKENS, D), 1.0, 6.0, ((0, 16), (1, 8)))
    doc_lengths = jax.vmap(lambda own: ragged(own, DOCS, TOKENS, LONGEST, 2))(jax.random.split(key_list[7], SEQS)).reshape((SEQS, DOCS)).astype(jnp.int32)
    return {"queries": queries, "keys": keys, "values": values, "directions": directions, "beta_logits": beta_logits, "out_proj": out_proj, "out_grad": out_grad, "doc_lengths": doc_lengths}


highest = lax.Precision.HIGHEST

def nudge(value):
    rounded = lax.optimization_barrier(value.astype(jnp.bfloat16)).astype(value.dtype)
    return value + lax.stop_gradient(rounded - value)

def block_parts(query, key_rows, direction, beta):
    size = query.shape[0]
    order = jnp.arange(size, dtype=jnp.int32)
    within = order[None, :] <= order[:, None]
    before = order[:, None] > order[None, :]
    gram = jnp.dot(direction, direction.T, precision=highest)
    unit = jnp.eye(size, dtype=query.dtype) + jnp.where(before, beta[:, None] * gram, 0.0)
    solved = jax.scipy.linalg.solve_triangular(unit, beta[:, None] * direction, lower=True, unit_diagonal=True)
    across = jnp.where(within, jnp.dot(query, direction.T, precision=highest), 0.0)
    query_bar = query - jnp.dot(across, solved, precision=highest)
    right = jnp.where(before, beta[:, None] * jnp.dot(direction, key_rows.T, precision=highest), 0.0)
    coeffs = jax.scipy.linalg.solve_triangular(unit, right, lower=True, unit_diagonal=True)
    key_tilde = key_rows - jnp.dot(coeffs.T, direction, precision=highest)
    inner = jnp.dot(query, key_rows.T, precision=highest) - jnp.dot(across, coeffs, precision=highest)
    transform = jnp.eye(direction.shape[1], dtype=query.dtype) - jnp.dot(direction.T, solved, precision=highest)
    return (query_bar, key_tilde, transform, inner)

def block_local(query, keys_in, raw_dirs, logits):
    size = query.shape[0]
    heads = logits.shape[0]

    def split(matrix):
        return matrix.reshape(size, heads, -1).transpose(1, 0, 2)
    direction = split(raw_dirs)
    direction = direction * lax.rsqrt(lax.optimization_barrier(jnp.sum(direction * direction, axis=-1, keepdims=True)) + 1e-06)
    beta = 2.0 * jax.nn.sigmoid(logits)
    return jax.vmap(block_parts)(split(query), split(keys_in), direction, beta)

def doc_ids(lengths, start, size):
    ends = jnp.cumsum(lengths)
    places = start + jnp.arange(size, dtype=jnp.int32)
    return lax.optimization_barrier(jnp.sum((ends[None, :] <= places[:, None]).astype(jnp.int32), axis=1))

def attend(query, keys_in, value, raw_dirs, logits, lengths):
    size = TOK_DEV
    blocks = query.shape[0] // size
    heads = logits.shape[0]
    hdim = query.shape[1] // heads
    scale = hdim ** (-0.5)
    parts = [block_local(query[b * size:(b + 1) * size], keys_in[b * size:(b + 1) * size], raw_dirs[b * size:(b + 1) * size], logits[:, b * size:(b + 1) * size]) for b in range(blocks)]
    mats = [nudge(part[2]) for part in parts]
    idents = [doc_ids(lengths, b * size, size) for b in range(blocks)]
    order = jnp.arange(size, dtype=jnp.int32)
    causal = order[None, :] <= order[:, None]
    chains = {}
    for source in range(blocks):
        carried = nudge(parts[source][1])
        for target in range(source + 1, blocks):
            chains[source, target] = carried
            carried = nudge(jnp.einsum('hlk,hmk->hlm', carried, mats[target], precision=highest))
    outputs = []
    for target in range(blocks):
        query_half = nudge(parts[target][0])
        same = idents[target][:, None] == idents[target][None, :]
        pieces = [jnp.where(causal & same, parts[target][3] * scale, -1e+30)]
        value_list = [value[target * size:(target + 1) * size]]
        for step in range(1, target + 1):
            source = target - step
            raw = jnp.einsum('hik,hjk->hij', query_half, chains[source, target], precision=highest) * scale
            seen = idents[target][:, None] == idents[source][None, :]
            pieces.append(jnp.where(seen, raw, -1e+30))
            value_list.append(value[source * size:(source + 1) * size])
        scores = jnp.concatenate(pieces, axis=2)
        probs = nudge(jax.nn.softmax(scores, axis=-1))
        stacked = jnp.concatenate(value_list, axis=0).reshape(-1, heads, hdim)
        outputs.append(jnp.einsum('hij,jhk->ihk', probs, stacked, precision=highest).reshape(size, -1))
    return jnp.concatenate(outputs, axis=0)

def reference(queries, keys, values, directions, beta_logits, out_proj, out_grad, doc_lengths):

    def one(carry, items):
        query, keys_in, value, raw_dirs, logits, grad_out, lengths = items
        dout = jnp.dot(grad_out.astype(jnp.float32), out_proj.T.astype(jnp.float32), preferred_element_type=jnp.float32).astype(jnp.bfloat16)

        def forward(first, second, third, fourth, fifth):
            return attend(first, second, third, fourth, fifth, lengths)
        output, pullback = jax.vjp(forward, query.astype(jnp.float32), keys_in.astype(jnp.float32), value.astype(jnp.float32), raw_dirs.astype(jnp.float32), logits)
        grads = pullback(dout.astype(jnp.float32))
        out_half = output.astype(jnp.bfloat16)
        carry = carry + jnp.dot(out_half.T.astype(jnp.float32), grad_out.astype(jnp.float32), preferred_element_type=jnp.float32)
        return (carry, (grads[0].astype(jnp.bfloat16), grads[1].astype(jnp.bfloat16), grads[2].astype(jnp.bfloat16), grads[3].astype(jnp.bfloat16), grads[4]))
    start = jnp.zeros((out_proj.shape[0], out_proj.shape[1]), jnp.float32)
    summed, each = lax.scan(one, start, (queries, keys, values, directions, beta_logits, out_grad, doc_lengths))
    return (each[0], each[1], each[2], each[3], each[4], summed)
```

```python
import functools

import jax
import jax.numpy as jnp
from jax import lax
from jax.experimental import pallas as pl
from jax.experimental.pallas import tpu as pltpu
from jax.sharding import PartitionSpec as P

f32, bf16 = jnp.float32, jnp.bfloat16
MESH = pl.DeviceIdType.MESH
N = 128
B = 8
TOKENS = N * B
WIDTH = 4096
SLICE = WIDTH // B
HALF = SLICE // 2
ROWS = 64
SCALE = N**-0.5
GROUP = 4
Q, K, U, V, DO = range(5)


def dot(a, b, ca, cb):
    return lax.dot_general(
        a.astype(bf16), b.astype(bf16), (((ca,), (cb,)), ((), ())), preferred_element_type=f32
    )


def nn(a, b):
    return dot(a, b, 1, 0)


def nt(a, b):
    return dot(a, b, 1, 1)


def tn(a, b):
    return dot(a, b, 0, 0)


def down(*parts):
    return jnp.concatenate(parts, 0)


def beside(*parts):
    return jnp.concatenate(parts, 1)


def split(x):
    high = x.astype(bf16)
    return high, (x - high.astype(f32)).astype(bf16)


def nn3(a, b):
    ah, al = split(a)
    bh, bl = split(b)
    return nn(beside(ah, al), down(bh, bh)) + nn(ah, bl)


def masks():
    row = lax.broadcasted_iota(jnp.int32, (N, N), 0)
    col = lax.broadcasted_iota(jnp.int32, (N, N), 1)
    return row, col, row == col, row > col, col <= row


def block_forward(query, keys, raw, logit):
    row, col, eye, before, within = masks()
    prods = nt(down(raw, query), down(raw, keys))
    yield
    uu, uk, qu, qk = prods[:N, :N], prods[:N, N:], prods[N:, :N], prods[N:, N:]
    diag = jnp.where(eye, uu, 0.0)
    r_row = lax.rsqrt(jnp.sum(diag, 0, keepdims=True) + 1e-6)
    r_col = lax.rsqrt(jnp.sum(diag, 1, keepdims=True) + 1e-6)
    b_row = 2.0 / (1.0 + jnp.exp(-logit))
    b_col = jnp.sum(jnp.where(eye, b_row, 0.0), 1, keepdims=True)
    br = b_col * r_col
    lower = jnp.where(before, br * uu * r_row, 0.0)
    right = jnp.where(before, br * uk, 0.0)
    across = jnp.where(within, qu * r_row, 0.0)
    inv = jnp.where(eye, 1.0, jnp.where((row >> 1) == (col >> 1), -lower, 0.0))
    for level in range(1, 7):
        mask = ((row >> (level + 1)) == (col >> (level + 1))) & ((row >> level) != (col >> level))
        half = nn3(inv, jnp.where(mask, lower, 0.0))
        yield
        inv = inv - nn3(half, inv)
        yield
    yc = nn3(inv, beside(br * raw.astype(f32), right))
    yield
    eyc = nn3(across, yc)
    yield
    query_bar = query.astype(f32) - eyc[:, :N]
    inner = qk - eyc[:, N:]
    high, low = split(yc * r_col)
    shift = tn(down(high, low), down(raw, raw))
    move = jnp.where(eye, 1.0, 0.0) - shift[:N]
    key_tilde = keys.astype(f32) - shift[N:]
    return dict(
        uu=uu, uk=uk, r_row=r_row, r_col=r_col, b_col=b_col, across=across.astype(bf16), inv=inv.astype(bf16),
        yc=yc.astype(bf16), qhat=query_bar.astype(bf16), move=move.astype(bf16), ktil=key_tilde.astype(bf16), inner=inner,
    )


def block_backward(query, keys, raw, f, d_inner, d_qbar, d_ktil, d_move):
    row, col, eye, before, within = masks()
    r_row, r_col, b_col, yc, across = f["r_row"], f["r_col"], f["b_col"], f["yc"], f["across"]
    w = raw.astype(f32) * r_col
    wb = w.astype(bf16)
    d_in = d_inner.astype(bf16)
    d_qi = beside(d_qbar.astype(bf16), d_in)
    d_mk = down(d_move, d_ktil).astype(bf16)
    d_yc = -(tn(across, d_qi) + nt(wb, d_mk))
    yield
    d_across = jnp.where(within, -nt(d_qi, yc), 0.0).astype(bf16)
    yield
    d_br = tn(f["inv"], d_yc)
    yield
    d_lower = jnp.where(before, -nt(d_br, yc), 0.0)
    yield
    d_bw, d_right = d_br[:, :N], jnp.where(before, d_br[:, N:], 0.0)
    d_beta = jnp.sum(
        d_right * (r_col * f["uk"]) + d_lower * (r_col * f["uu"] * r_row) + d_bw * w, 1, keepdims=True
    )
    d_wk = (b_col * d_right).astype(bf16)
    d_gram = (b_col * d_lower).astype(bf16)
    kw, qw = down(keys, wb), down(query, wb)
    d_query = d_qbar + nn(beside(d_in, d_across), kw)
    yield
    d_keys = d_ktil + tn(down(d_in, d_wk), qw)
    yield
    d_w = b_col * d_bw - nn(yc, d_mk) + nn(beside(d_wk, d_gram), kw) + tn(down(d_across, d_gram), qw)
    yield
    d_raw = r_col * (d_w - w * jnp.sum(w * d_w, 1, keepdims=True))
    d_logit = d_beta * b_col * (1.0 - 0.5 * b_col)
    d_logit = jnp.sum(jnp.where(eye, d_logit, 0.0), 0, keepdims=True)
    return d_query.astype(bf16), d_keys.astype(bf16), d_raw.astype(bf16), d_logit


def together(steps):
    steps = list(steps)
    results = [None] * len(steps)
    live = list(range(len(steps)))
    while live:
        for i in list(live):
            try:
                next(steps[i])
            except StopIteration as stop:
                results[i] = stop.value
                live.remove(i)
    return results


def kernel(
    lens, q_in, k_in, v_in, u_in, l_in, proj, grad,
    dq_out, dk_out, dv_out, du_out, gp_out, dl_out,
    ins, logits, grad_own, proj_own, dout_own, grad_cut, att, made, dl_made, dl_got, prod, rs_first, mid, rs_last, fin,
    in_send, in_recv, out_send, out_recv, att_send, att_recv, rs_send, rs_recv, fin_send, fin_recv, here,
):
    dp, me = lax.axis_index("dp"), lax.axis_index("ctx")
    py, pz = lax.div(dp, 4), lax.rem(dp, 4)
    sibling = me + 1 - 2 * lax.rem(me, 2)
    peers = [lax.rem(me + o, B) for o in range(B)]
    along_y = [(lax.rem(py + o, 4), (lax.rem(py + o, 4) * 4 + pz, me)) for o in range(4)]
    along_z = [(lax.rem(pz + o, 4), (py * 4 + lax.rem(pz + o, 4), me)) for o in range(4)]
    rows = pl.ds(pl.multiple_of(me * N, N), N)

    def cols(p, width=N):
        return pl.ds(pl.multiple_of(p * width, width), width)

    sent = []

    def send(src, dst, send_sem, recv_sem, device):
        copy = pltpu.make_async_remote_copy(
            src_ref=src, dst_ref=dst, send_sem=send_sem, recv_sem=recv_sem, device_id=device, device_id_type=MESH
        )
        copy.start()
        sent.append(copy)
        return copy

    def local(src, dst, sem):
        copy = pltpu.make_async_copy(src, dst, sem)
        copy.start()
        return copy

    sources = {Q: q_in, K: k_in, U: u_in, V: v_in}
    own = [local(ref.at[0, :, cols(me)], ins.at[a, rows], here.at[a]) for a, ref in sources.items()]
    own.append(local(l_in.at[0], logits.at[me], here.at[4]))
    own_grad = local(grad.at[0], grad_own, here.at[5])
    own_cut = local(grad.at[0, :, cols(me, SLICE)], grad_cut.at[rows], here.at[6])
    own_proj = [local(proj.at[cols(peers[o])], proj_own.at[o], here.at[8 + o]) for o in range(B)]

    barrier = pltpu.get_barrier_semaphore()
    greeted = [(dp, p) for p in peers[1:]] + [d for _, d in along_y[1:]] + [d for _, d in along_z[1:]]
    for device in greeted:
        pl.semaphore_signal(barrier, inc=1, device_id=device, device_id_type=MESH)
    pl.semaphore_wait(barrier, len(greeted))

    got = {}
    for a in (U, K, Q, 5, V):
        for o in range(1, B):
            to = (dp, peers[o])
            if a == 5:
                got[a, o] = send(l_in.at[0], logits.at[me], in_send.at[a, o], in_recv.at[a, o], to)
            else:
                got[a, o] = send(
                    sources[a].at[0, :, cols(peers[o])], ins.at[a, rows], in_send.at[a, o], in_recv.at[a, o], to
                )

    own_grad.wait()
    for o in [*range(1, B), 0]:
        own_proj[o].wait()
        dout_own[o] = nt(grad_own[...], proj_own[o]).astype(bf16)
        if o:
            got[DO, o] = send(dout_own.at[o], ins.at[DO, rows], in_send.at[DO, o], in_recv.at[DO, o], (dp, peers[o]))
    own_dout = local(dout_own.at[0], ins.at[DO, rows], here.at[7])
    for o in range(1, B):
        got[6, o] = send(
            grad.at[0, :, cols(peers[o], SLICE)], grad_cut.at[rows], in_send.at[6, o], in_recv.at[6, o], (dp, peers[o])
        )

    for copy in own:
        copy.wait()
    for a in (U, K, Q, 5):
        for o in range(1, B):
            got[a, o].wait_recv()

    def block(a, c):
        return ins[a, c * N : (c + 1) * N]

    head = lax.broadcasted_iota(jnp.int32, (B, N), 0) == me
    f = []
    for g in range(0, B, GROUP):
        f += together(
            block_forward(
                block(Q, c), block(K, c), block(U, c), jnp.sum(jnp.where(head, logits[c], 0.0), 0, keepdims=True)
            )
            for c in range(g, g + GROUP)
        )
    carried = [None]
    for c in range(1, B):
        new = f[c - 1]["ktil"]
        carried.append(new if c == 1 else down(nn(carried[c - 1], f[c - 1]["move"]).astype(bf16), new))

    for o in range(1, B):
        got[V, o].wait_recv()
    ends = [lens[0, 0]]
    for i in range(1, 4):
        ends.append(ends[-1] + lens[0, i])
    probs = []
    for c in range(B):
        span = (c + 1) * N
        place = lax.broadcasted_iota(jnp.int32, (N, 1), 0) + c * N
        start = jnp.zeros((N, 1), jnp.int32)
        for end in ends:
            start = jnp.where(end <= place, jnp.maximum(start, end), start)
        key_place = lax.broadcasted_iota(jnp.int32, (N, span), 1)
        seen = (key_place >= start) & (key_place <= place)
        raw = f[c]["inner"] if c == 0 else beside(nt(f[c]["qhat"], carried[c]), f[c]["inner"])
        score = jnp.where(seen, raw * SCALE, -1e30)
        part = jnp.exp(score - jnp.max(score, 1, keepdims=True))
        prob = part / jnp.sum(part, 1, keepdims=True)
        probs.append(prob)
        att[me, c * N : (c + 1) * N] = nn(prob, ins[V, :span]).astype(bf16)

    att_got = []
    for i, o in enumerate((2, 4, 6)):
        att_got.append(send(att.at[me], att.at[me], att_send.at[i], att_recv.at[i], (dp, peers[o])))
    att_got.append(send(att.at[me], att.at[me], att_send.at[3], att_recv.at[3], (dp, sibling)))

    own_dout.wait()
    for o in range(1, B):
        got[DO, o].wait_recv()
    d_inner, d_qbar, d_carried = [], [], [None] * B
    d_value = [None] * B
    for c in range(B):
        span = (c + 1) * N
        grads = block(DO, c)
        prob = probs[c]
        d_prob = nt(grads, ins[V, :span])
        d_score = prob * (d_prob - jnp.sum(prob * d_prob, 1, keepdims=True)) * SCALE
        term = tn(prob, grads)
        for j in range(c + 1):
            piece = term[j * N : (j + 1) * N]
            d_value[j] = piece if j == c else d_value[j] + piece
        d_inner.append(d_score[:, c * N :])
        if c:
            early = d_score[:, : c * N].astype(bf16)
            d_qbar.append(nn(early, carried[c]))
            d_carried[c] = tn(early, f[c]["qhat"])
        else:
            d_qbar.append(jnp.zeros((N, N), f32))
    out = {}

    def send_made(i, result):
        out[i, 0] = local(made.at[i, rows], result.at[0, :, cols(me)], here.at[16 + i])
        for o in range(1, B):
            out[i, o] = send(
                made.at[i, cols(peers[o])], result.at[0, :, cols(me)], out_send.at[i, o], out_recv.at[i, o], (dp, peers[o])
            )

    for j in range(B):
        made[3, j * N : (j + 1) * N] = d_value[j].astype(bf16)
    send_made(3, dv_out)

    d_ktil = [None] * (B - 1) + [jnp.zeros((N, N), f32)]
    d_move = [jnp.zeros((N, N), f32)] * B
    later = None
    for c in range(B - 1, 0, -1):
        now = d_carried[c]
        if later is not None:
            back = later[: c * N].astype(bf16)
            now = now + nt(back, f[c]["move"])
            d_move[c] = tn(carried[c], back)
        d_ktil[c - 1] = now[(c - 1) * N :]
        later = now

    for i, o in enumerate((2, 4, 6)):
        att_got[i].wait_recv()
        source = lax.rem(me + B - o, B)
        att_got.append(send(att.at[source], att.at[source], att_send.at[4 + i], att_recv.at[4 + i], (dp, sibling)))

    for g in range(0, B, GROUP):
        results = together(
            block_backward(
                block(Q, c), block(K, c), block(U, c), f[c], d_inner[c], d_qbar[c], d_ktil[c], d_move[c]
            )
            for c in range(g, g + GROUP)
        )
        for c, (d_query, d_keys, d_raw, d_logit) in zip(range(g, g + GROUP), results):
            made[0, c * N : (c + 1) * N] = d_query
            made[1, c * N : (c + 1) * N] = d_keys
            made[2, c * N : (c + 1) * N] = d_raw
            dl_made[c] = jnp.where(head, d_logit, 0.0)
    send_made(0, dq_out)
    send_made(1, dk_out)
    send_made(2, du_out)
    out[4, 0] = local(dl_made.at[me], dl_got.at[me], here.at[20])
    for o in range(1, B):
        out[4, o] = send(
            dl_made.at[peers[o]], dl_got.at[me], out_send.at[4, o], out_recv.at[4, o], (dp, peers[o])
        )

    own_cut.wait()
    for o in range(1, B):
        got[6, o].wait_recv()
    for copy in att_got[3:]:
        copy.wait_recv()
    for h in range(B):
        term = tn(att[h], grad_cut[...]).astype(bf16)
        prod[h // 2, 2 * (h % 2)] = term[:ROWS]
        prod[h // 2, 2 * (h % 2) + 1] = term[ROWS:]

    left, right = pl.ds(0, HALF), pl.ds(HALF, HALF)
    first = []
    for o in range(1, 4):
        jy, dev_y = along_y[o]
        first.append(
            send(prod.at[jy, :, :, left], rs_first.at[0, o - 1], rs_send.at[0, o], rs_recv.at[0, o], dev_y)
        )
        jz, dev_z = along_z[o]
        first.append(
            send(prod.at[:, jz, :, right], rs_first.at[1, o - 1], rs_send.at[1, o], rs_recv.at[1, o], dev_z)
        )
    for copy in first:
        copy.wait_recv()
    mid[0] = (prod[py, :, :, :HALF].astype(f32) + sum(rs_first[0, i].astype(f32) for i in range(3))).astype(bf16)
    mid[1] = (prod[:, pz, :, HALF:].astype(f32) + sum(rs_first[1, i].astype(f32) for i in range(3))).astype(bf16)
    last = []
    for o in range(1, 4):
        jz, dev_z = along_z[o]
        last.append(send(mid.at[0, jz], rs_last.at[0, o - 1], rs_send.at[2, o], rs_recv.at[2, o], dev_z))
        jy, dev_y = along_y[o]
        last.append(send(mid.at[1, jy], rs_last.at[1, o - 1], rs_send.at[3, o], rs_recv.at[3, o], dev_y))
    for copy in last:
        copy.wait_recv()
    total = beside(
        mid[0, pz].astype(f32) + sum(rs_last[0, i].astype(f32) for i in range(3)),
        mid[1, py].astype(f32) + sum(rs_last[1, i].astype(f32) for i in range(3)),
    )
    for p in range(B):
        fin[p] = total[p * 8 : (p + 1) * 8]
    gp_own = local(fin.at[me], gp_out.at[:, cols(me, SLICE)], here.at[21])
    gp_got = [
        send(fin.at[peers[o]], gp_out.at[:, cols(me, SLICE)], fin_send.at[o], fin_recv.at[o], (dp, peers[o]))
        for o in range(1, B)
    ]

    for i in range(5):
        out[i, 0].wait()
        for o in range(1, B):
            out[i, o].wait_recv()
    dl_out[0] = sum(dl_got[h] for h in range(B))
    gp_own.wait()
    for copy in gp_got:
        copy.wait_recv()
    for copy in sent:
        copy.wait_send()


def per_device(queries, keys, values, directions, beta_logits, out_proj, out_grad, doc_lengths):
    tokens = jax.ShapeDtypeStruct((1, N, TOKENS), bf16)
    anywhere = pl.BlockSpec(memory_space=pl.ANY)
    dma = pltpu.SemaphoreType.DMA
    dq, dk, dv, du, gp, dl = pl.pallas_call(
        kernel,
        out_shape=[tokens] * 4
        + [jax.ShapeDtypeStruct((B, WIDTH), f32), jax.ShapeDtypeStruct((1, B, N), f32)],
        in_specs=[pl.BlockSpec(memory_space=pltpu.SMEM)] + [anywhere] * 7,
        out_specs=[anywhere] * 5 + [pl.BlockSpec(memory_space=pltpu.VMEM)],
        scratch_shapes=[
            pltpu.VMEM((5, TOKENS, N), bf16),
            pltpu.VMEM((B, B, N), f32),
            pltpu.VMEM((N, WIDTH), bf16),
            pltpu.VMEM((B, N, WIDTH), bf16),
            pltpu.VMEM((B, N, N), bf16),
            pltpu.VMEM((TOKENS, SLICE), bf16),
            pltpu.VMEM((B, TOKENS, N), bf16),
            pltpu.VMEM((4, TOKENS, N), bf16),
            pltpu.VMEM((B, B, N), f32),
            pltpu.VMEM((B, B, N), f32),
            pltpu.VMEM((4, 4, ROWS, SLICE), bf16),
            pltpu.VMEM((2, 3, 4, ROWS, HALF), bf16),
            pltpu.VMEM((2, 4, ROWS, HALF), bf16),
            pltpu.VMEM((2, 3, ROWS, HALF), bf16),
            pltpu.VMEM((B, B, SLICE), f32),
            dma((7, B)),
            dma((7, B)),
            dma((5, B)),
            dma((5, B)),
            dma((7,)),
            dma((7,)),
            dma((4, 4)),
            dma((4, 4)),
            dma((B,)),
            dma((B,)),
            dma((22,)),
        ],
        compiler_params=pltpu.CompilerParams(
            collective_id=0, has_side_effects=True, vmem_limit_bytes=56 * 2**20
        ),
    )(doc_lengths, queries, keys, values, directions, beta_logits, out_proj, out_grad)
    return dq, dk, dv, du, dl, gp


def solution(mesh):
    rows = P("dp", "ctx", None)
    return jax.shard_map(
        per_device,
        mesh=mesh,
        in_specs=(rows, rows, rows, rows, P("dp", None, "ctx"), P(), rows, P("dp", None)),
        out_specs=(rows, rows, rows, rows, P("dp", None, "ctx"), P(("dp", "ctx"), None)),
        check_vma=False,
    )
```

```python
import functools

import jax
import jax.numpy as jnp
from jax import lax
from jax.experimental import pallas as pl
from jax.experimental.pallas import tpu as pltpu
from jax.sharding import PartitionSpec as P

f32, bf16 = jnp.float32, jnp.bfloat16
MESH = pl.DeviceIdType.MESH
N = 128
B = 8
TOKENS = N * B
WIDTH = 4096
PART = WIDTH // 4
SCALE = N**-0.5
Q, K, U, V, DO = range(5)
FIELDS = {
    "uu": ((N, N), f32), "uk": ((N, N), f32), "inner": ((N, N), f32), "r_row": ((1, N), f32), "r_col": ((N, 1), f32),
    "b_col": ((N, 1), f32), "across": ((N, N), bf16), "inv": ((N, N), bf16), "yc": ((N, 2 * N), bf16),
    "qhat": ((N, N), bf16), "move": ((N, N), bf16), "ktil": ((N, N), bf16), "d_inner": ((N, N), bf16),
    "d_qbar": ((N, N), f32), "d_ktil": ((N, N), f32), "d_move": ((N, N), bf16),
}
NEAR, NEXT, FAR = (1,), (2, 3, 6, 7), (4, 5)


def dot(a, b, ca, cb):
    return lax.dot_general(
        a.astype(bf16), b.astype(bf16), (((ca,), (cb,)), ((), ())), preferred_element_type=f32
    )


def nn(a, b):
    return dot(a, b, 1, 0)


def nt(a, b):
    return dot(a, b, 1, 1)


def tn(a, b):
    return dot(a, b, 0, 0)


def down(*parts):
    return jnp.concatenate(parts, 0)


def beside(*parts):
    return jnp.concatenate(parts, 1)


def split(x):
    high = x.astype(bf16)
    return high, (x - high.astype(f32)).astype(bf16)


def nn3(a, b):
    ah, al = split(a)
    bh, bl = split(b)
    return nn(beside(ah, al), down(bh, bh)) + nn(ah, bl)


def masks():
    row = lax.broadcasted_iota(jnp.int32, (N, N), 0)
    col = lax.broadcasted_iota(jnp.int32, (N, N), 1)
    return row, col, row == col, row > col, col <= row


def block_forward(c, ins, logit, f):
    query, keys, raw = (ins[a, pl.ds(c * N, N)] for a in (Q, K, U))
    row, col, eye, before, within = masks()
    prods = nt(down(raw, query), down(raw, keys))
    yield
    uu, uk, qu, qk = prods[:N, :N], prods[:N, N:], prods[N:, :N], prods[N:, N:]
    diag = jnp.where(eye, uu, 0.0)
    r_row = lax.rsqrt(jnp.sum(diag, 0, keepdims=True) + 1e-6)
    r_col = lax.rsqrt(jnp.sum(diag, 1, keepdims=True) + 1e-6)
    b_row = 2.0 / (1.0 + jnp.exp(-logit))
    b_col = jnp.sum(jnp.where(eye, b_row, 0.0), 1, keepdims=True)
    br = b_col * r_col
    lower = jnp.where(before, br * uu * r_row, 0.0)
    right = jnp.where(before, br * uk, 0.0)
    across = jnp.where(within, qu * r_row, 0.0)
    inv = jnp.where(eye, 1.0, jnp.where((row >> 1) == (col >> 1), -lower, 0.0))
    for level in range(1, 7):
        mask = ((row >> (level + 1)) == (col >> (level + 1))) & ((row >> level) != (col >> level))
        half = nn3(inv, jnp.where(mask, lower, 0.0))
        yield
        inv = inv - nn3(half, inv)
        yield
    yc = nn3(inv, beside(br * raw.astype(f32), right))
    yield
    eyc = nn3(across, yc)
    yield
    query_bar = query.astype(f32) - eyc[:, :N]
    inner = qk - eyc[:, N:]
    high, low = split(yc * r_col)
    shift = tn(down(high, low), down(raw, raw))
    move = jnp.where(eye, 1.0, 0.0) - shift[:N]
    key_tilde = keys.astype(f32) - shift[N:]
    f["uu"][c], f["uk"][c], f["r_row"][c], f["r_col"][c], f["b_col"][c] = uu, uk, r_row, r_col, b_col
    f["across"][c], f["inv"][c], f["yc"][c] = across.astype(bf16), inv.astype(bf16), yc.astype(bf16)
    f["qhat"][c], f["move"][c], f["ktil"][c] = query_bar.astype(bf16), move.astype(bf16), key_tilde.astype(bf16)
    f["inner"][c] = inner


def block_backward(c, ins, f):
    query, keys, raw = (ins[a, pl.ds(c * N, N)] for a in (Q, K, U))
    row, col, eye, before, within = masks()
    r_row, r_col, b_col, yc, across = (f[name][c] for name in ("r_row", "r_col", "b_col", "yc", "across"))
    d_in, d_qbar, d_ktil = f["d_inner"][c], f["d_qbar"][c], f["d_ktil"][c]
    w = raw.astype(f32) * r_col
    wb = w.astype(bf16)
    d_qi = beside(d_qbar.astype(bf16), d_in)
    d_mk = down(f["d_move"][c], d_ktil.astype(bf16))
    d_yc = -(tn(across, d_qi) + nt(wb, d_mk))
    yield
    d_across = jnp.where(within, -nt(d_qi, yc), 0.0).astype(bf16)
    yield
    d_br = tn(f["inv"][c], d_yc)
    yield
    d_lower = jnp.where(before, -nt(d_br, yc), 0.0)
    yield
    d_bw, d_right = d_br[:, :N], jnp.where(before, d_br[:, N:], 0.0)
    d_beta = jnp.sum(
        d_right * (r_col * f["uk"][c]) + d_lower * (r_col * f["uu"][c] * r_row) + d_bw * w, 1, keepdims=True
    )
    d_wk = (b_col * d_right).astype(bf16)
    d_gram = (b_col * d_lower).astype(bf16)
    kw, qw = down(keys, wb), down(query, wb)
    d_query = d_qbar + nn(beside(d_in, d_across), kw)
    yield
    d_keys = d_ktil + tn(down(d_in, d_wk), qw)
    yield
    d_w = b_col * d_bw - nn(yc, d_mk) + nn(beside(d_wk, d_gram), kw) + tn(down(d_across, d_gram), qw)
    yield
    d_raw = r_col * (d_w - w * jnp.sum(w * d_w, 1, keepdims=True))
    d_logit = d_beta * b_col * (1.0 - 0.5 * b_col)
    d_logit = jnp.sum(jnp.where(eye, d_logit, 0.0), 0, keepdims=True)
    return d_query.astype(bf16), d_keys.astype(bf16), d_raw.astype(bf16), d_logit


def together(steps):
    steps = list(steps)
    results = [None] * len(steps)
    live = list(range(len(steps)))
    while live:
        for i in list(live):
            try:
                next(steps[i])
            except StopIteration as stop:
                results[i] = stop.value
                live.remove(i)
    return results


def kernel(
    lens, q_in, k_in, v_in, u_in, l_in, proj, grad,
    dq_out, dk_out, dv_out, du_out, gp_out, dl_out,
    ins, logits, grad_own, proj_own, dout_own, grad_z, grad_y, att_own, att, att_z, att_y, made, dl_made, dl_got, prod, rs_first, mid, rs_last, fin,
    in_send, in_recv, out_send, out_recv, att_send, att_recv, rs_send, rs_recv, fin_send, fin_recv, here, *parts,
):
    f = dict(zip(FIELDS, parts))
    dp, me = lax.axis_index("dp"), lax.axis_index("ctx")
    py, pz = lax.div(dp, 4), lax.rem(dp, 4)
    sibling = me + 1 - 2 * lax.rem(me, 2)
    px, core = lax.div(me, 2), lax.rem(me, 2)
    y_at = [lax.rem(py + o, 4) for o in range(4)]
    z_at = [lax.rem(pz + o, 4) for o in range(4)]
    x_at = [lax.rem(px + o, 4) for o in range(4)]
    peers = [x_at[o // 2] * 2 + lax.rem(core + o % 2, 2) for o in range(B)]
    along_y = [(y * 4 + pz, me) for y in y_at]
    along_z = [(py * 4 + z, me) for z in z_at]
    along_x = [(dp, x * 2 + core) for x in x_at]
    z_slot, y_slot = pz * 2 + core, py * 2 + core
    z_group = [(c, (py * 4 + z, px * 2 + c), z) for z in z_at for c in (core, 1 - core)]
    y_group = [(c, (y * 4 + pz, px * 2 + c), y) for y in y_at for c in (core, 1 - core)]
    rows = pl.ds(pl.multiple_of(me * N, N), N)

    def cols(p, width=N):
        return pl.ds(pl.multiple_of(p * width, width), width)

    sent = []

    def send(src, dst, send_sem, recv_sem, device):
        copy = pltpu.make_async_remote_copy(
            src_ref=src, dst_ref=dst, send_sem=send_sem, recv_sem=recv_sem, device_id=device, device_id_type=MESH
        )
        copy.start()
        sent.append(copy)
        return copy

    def local(src, dst, sem):
        copy = pltpu.make_async_copy(src, dst, sem)
        copy.start()
        return copy

    sources = {Q: q_in, K: k_in, U: u_in, V: v_in}
    own = [local(ref.at[0, :, cols(me)], ins.at[a, rows], here.at[a]) for a, ref in sources.items()]
    own.append(local(l_in.at[0], logits.at[me], here.at[4]))
    own_grad = local(grad.at[0], grad_own, here.at[5])
    z_rows, y_rows = (pl.ds(pl.multiple_of(slot * N, N), N) for slot in (z_slot, y_slot))
    own_cut = [
        local(grad.at[0, :, cols(core, PART)], grad_z.at[z_rows], here.at[6]),
        local(grad.at[0, :, cols(core + 2, PART)], grad_y.at[y_rows], here.at[22]),
    ]
    own_proj = [local(proj.at[cols(x_at[dx], 2 * N)], proj_own.at[dx], here.at[8 + dx]) for dx in range(4)]

    barrier = pltpu.get_barrier_semaphore()
    greeted = [(dp, p) for p in peers[1:]] + [d for _, d, _ in y_group[2:] + z_group[2:]]
    for device in greeted:
        pl.semaphore_signal(barrier, inc=1, device_id=device, device_id_type=MESH)
    pl.semaphore_wait(barrier, len(greeted))

    got = {}

    def send_in(a, o):
        if a == 5:
            src, dst = l_in.at[0], logits.at[me]
        else:
            src, dst = sources[a].at[0, :, cols(peers[o])], ins.at[a, rows]
        got[a, o] = send(src, dst, in_send.at[a, o], in_recv.at[a, o], (dp, peers[o]))

    for near in (NEAR, NEXT, FAR):
        for a in (U, K, Q, 5):
            for o in near:
                send_in(a, o)
    for o in (*NEXT, *FAR, *NEAR):
        send_in(V, o)

    for o in range(1, B):
        c, to, _ = z_group[o]
        got[6, o] = send(grad.at[0, :, cols(c, PART)], grad_z.at[z_rows], in_send.at[6, o], in_recv.at[6, o], to)
        c, to, _ = y_group[o]
        got[7, o] = send(grad.at[0, :, cols(c + 2, PART)], grad_y.at[y_rows], in_send.at[7, o], in_recv.at[7, o], to)

    for copy in own:
        copy.wait()
    head = lax.broadcasted_iota(jnp.int32, (B, N), 0) == me

    def forward_of(blocks, arrivals):
        for a in (U, K, Q, 5):
            for o in arrivals:
                got[a, o].wait_recv()
        own_logits = [jnp.sum(jnp.where(head, logits[c], 0.0), 0, keepdims=True) for c in blocks]
        together(block_forward(c, ins, logit, f) for c, logit in zip(blocks, own_logits))

    forward_of([peers[o] for o in (0, 1)], NEAR)

    own_grad.wait()
    for dx in (1, 3, 2, 0):
        own_proj[dx].wait()
        both = nt(grad_own[...], proj_own[dx]).astype(bf16)
        for c in range(2):
            dout_own[dx, c] = both[:, c * N : (c + 1) * N]
        for o in (2 * dx, 2 * dx + 1):
            if o:
                src = dout_own.at[dx, lax.rem(peers[o], 2)]
                got[DO, o] = send(src, ins.at[DO, rows], in_send.at[DO, o], in_recv.at[DO, o], (dp, peers[o]))
    own_dout = local(dout_own.at[0, core], ins.at[DO, rows], here.at[7])

    forward_of([peers[o] for o in NEXT + FAR], NEXT + FAR)

    def block(a, c):
        return ins[a, c * N : (c + 1) * N]

    for o in range(1, B):
        got[V, o].wait_recv()
    ends = [lens[0, 0]]
    for i in range(1, 4):
        ends.append(ends[-1] + lens[0, i])
    carried, probs = [None] * B, [None] * B

    def carry_on():
        for c in range(1, B):
            new = f["ktil"][c - 1]
            carried[c] = new if c == 1 else down(nn(carried[c - 1], f["move"][c - 1]).astype(bf16), new)
            yield

    def row_forward(c):
        for _ in range(c):
            yield
        span = (c + 1) * N
        place = lax.broadcasted_iota(jnp.int32, (N, 1), 0) + c * N
        start = jnp.zeros((N, 1), jnp.int32)
        for end in ends:
            start = jnp.where(end <= place, jnp.maximum(start, end), start)
        key_place = lax.broadcasted_iota(jnp.int32, (N, span), 1)
        seen = (key_place >= start) & (key_place <= place)
        raw = f["inner"][c] if c == 0 else beside(nt(f["qhat"][c], carried[c]), f["inner"][c])
        yield
        score = jnp.where(seen, raw * SCALE, -1e30)
        peak = jnp.max(score, 1, keepdims=True)
        yield
        part = jnp.exp(score - peak)
        mass = jnp.sum(part, 1, keepdims=True)
        yield
        probs[c] = part * (1.0 / mass)
        result = nn(probs[c], ins[V, :span])
        yield
        att_own[c] = result.T.astype(bf16).reshape(2, 64, N)

    together([carry_on(), *(row_forward(c) for c in range(B))])

    own_att = local(att_own.at[me], att.at[lax.div(me, 2), pl.ds(lax.rem(me, 2) * 2, 2)], here.at[23])
    att_got = []
    for o in range(1, B):
        att_got.append(
            send(
                att_own.at[peers[o]], att.at[lax.div(me, 2), pl.ds(lax.rem(me, 2) * 2, 2)],
                att_send.at[0, o], att_recv.at[0, o], (dp, peers[o]),
            )
        )

    own_dout.wait()
    for o in range(1, B):
        got[DO, o].wait_recv()
    d_carried, d_value = [None] * B, [None] * B

    def row_backward(c):
        for _ in range(B - 1 - c):
            yield
        span = (c + 1) * N
        grads, prob = block(DO, c), probs[c]
        d_prob = nt(grads, ins[V, :span])
        yield
        mean = jnp.sum(prob * d_prob, 1, keepdims=True)
        yield
        d_score = prob * (d_prob - mean) * SCALE
        f["d_inner"][c] = d_score[:, c * N :].astype(bf16)
        if c:
            early = d_score[:, : c * N].astype(bf16)
            d_carried[c] = tn(early, f["qhat"][c])
            yield
            f["d_qbar"][c] = nn(early, carried[c])
        else:
            f["d_qbar"][c] = jnp.zeros((N, N), f32)
        yield
        term = tn(prob, grads)
        for j in range(c + 1):
            piece = term[j * N : (j + 1) * N]
            d_value[j] = piece if d_value[j] is None else d_value[j] + piece

    def carry_back():
        f["d_ktil"][B - 1] = jnp.zeros((N, N), f32)
        for c in (0, B - 1):
            f["d_move"][c] = jnp.zeros((N, N), bf16)
        later = None
        for c in range(B - 1, 0, -1):
            while d_carried[c] is None:
                yield
            now = d_carried[c]
            if later is not None:
                back = later[: c * N].astype(bf16)
                now = now + nt(back, f["move"][c])
                f["d_move"][c] = tn(carried[c], back).astype(bf16)
            f["d_ktil"][c - 1] = now[(c - 1) * N :]
            later = now
            yield

    together([*(row_backward(c) for c in range(B - 1, -1, -1)), carry_back()])

    out = {}
    results = (dq_out, dk_out, du_out, dv_out)

    def send_out(i, o):
        src, dst = made.at[i, cols(peers[o])], results[i].at[0, :, cols(me)]
        if o:
            out[i, o] = send(src, dst, out_send.at[i, o], out_recv.at[i, o], (dp, peers[o]))
        else:
            out[i, o] = local(src, dst, here.at[16 + i])

    for j in range(B):
        made[3, j * N : (j + 1) * N] = d_value[j].astype(bf16)
    for o in (*NEXT, *FAR, *NEAR, 0):
        send_out(3, o)

    own_att.wait()
    for copy in att_got:
        copy.wait_recv()
    own_share = [
        local(att.at[:, pz], att_z.at[z_slot], here.at[24]),
        local(att.at[py], att_y.at[y_slot], here.at[25]),
    ]
    shared = []
    for o in range(1, B):
        _, to, z = z_group[o]
        shared.append(send(att.at[:, z], att_z.at[z_slot], att_send.at[1, o], att_recv.at[1, o], to))
        _, to, y = y_group[o]
        shared.append(send(att.at[y], att_y.at[y_slot], att_send.at[2, o], att_recv.at[2, o], to))

    for some in (NEXT, FAR + (1, 0)):
        blocks = [peers[o] for o in some]
        for o, c, result in zip(some, blocks, together(block_backward(c, ins, f) for c in blocks)):
            for i in range(3):
                made[i, cols(c)] = result[i]
            dl_made[c] = jnp.where(head, result[3], 0.0)
            for i in range(3):
                send_out(i, o)
            if o:
                out[4, o] = send(dl_made.at[c], dl_got.at[me], out_send.at[4, o], out_recv.at[4, o], (dp, c))
            else:
                out[4, o] = local(dl_made.at[c], dl_got.at[me], here.at[20])

    for copy in own_cut + own_share:
        copy.wait()
    for o in range(1, B):
        got[6, o].wait_recv()
        got[7, o].wait_recv()
    for copy in shared:
        copy.wait_recv()
    for i, (left, right) in enumerate(((att_z, grad_z), (att_y, grad_y))):
        rows_of = beside(*(left[m].reshape(2 * N, N) for m in range(B)))
        prod[i] = nn(rows_of, right[...]).astype(bf16).reshape(4, 64, PART)

    first = []
    for o in range(1, 4):
        first.append(send(prod.at[0, y_at[o]], rs_first.at[0, o - 1], rs_send.at[0, o], rs_recv.at[0, o], along_y[o]))
        first.append(send(prod.at[1, z_at[o]], rs_first.at[1, o - 1], rs_send.at[1, o], rs_recv.at[1, o], along_z[o]))
    for copy in first:
        copy.wait_recv()
    for i, own in enumerate((py, pz)):
        part = prod[i, own].astype(f32) + sum(rs_first[i, o].astype(f32) for o in range(3))
        mid[:, i] = part.astype(bf16).reshape(4, 16, PART)
    last = []
    for o in range(1, 4):
        last.append(send(mid.at[x_at[o]], rs_last.at[o - 1], rs_send.at[2, o], rs_recv.at[2, o], along_x[o]))
    for copy in last:
        copy.wait_recv()
    total = mid[px].astype(f32) + sum(rs_last[o].astype(f32) for o in range(3))
    for c in range(2):
        fin[c] = total[:, c * 8 : c * 8 + 8]
    gp_own, gp_got = [], []
    for i in range(2):
        place = cols(core + 2 * i, PART)
        gp_own.append(local(fin.at[core, i], gp_out.at[:, place], here.at[26 + i]))
        gp_got.append(
            send(fin.at[1 - core, i], gp_out.at[:, place], fin_send.at[i], fin_recv.at[i], (dp, sibling))
        )

    for i in range(5):
        out[i, 0].wait()
        for o in range(1, B):
            out[i, o].wait_recv()
    dl_out[0] = sum(dl_got[h] for h in range(B))
    for copy in gp_own:
        copy.wait()
    for copy in gp_got:
        copy.wait_recv()
    for copy in sent:
        copy.wait_send()


def hand_over(*refs):
    count = (len(refs) - 1) // 2
    sems = refs[-1]
    copies = [pltpu.make_async_copy(refs[i], refs[count + i], sems.at[i]) for i in range(count)]
    for copy in copies:
        copy.start()
    for copy in copies:
        copy.wait()


def per_device(queries, keys, values, directions, beta_logits, out_proj, out_grad, doc_lengths):
    tokens = jax.ShapeDtypeStruct((1, N, TOKENS), bf16)
    anywhere = pl.BlockSpec(memory_space=pl.ANY)
    dma = pltpu.SemaphoreType.DMA
    results = [tokens] * 4 + [jax.ShapeDtypeStruct((B, WIDTH), f32), jax.ShapeDtypeStruct((1, B, N), f32)]
    made = pl.pallas_call(
        kernel,
        out_shape=results,
        in_specs=[pl.BlockSpec(memory_space=pltpu.SMEM)] + [anywhere] * 7,
        out_specs=[anywhere] * 5 + [pl.BlockSpec(memory_space=pltpu.VMEM)],
        scratch_shapes=[
            pltpu.VMEM((5, TOKENS, N), bf16),
            pltpu.VMEM((B, B, N), f32),
            pltpu.VMEM((N, WIDTH), bf16),
            pltpu.VMEM((4, 2 * N, WIDTH), bf16),
            pltpu.VMEM((4, 2, N, N), bf16),
            pltpu.VMEM((TOKENS, PART), bf16),
            pltpu.VMEM((TOKENS, PART), bf16),
            pltpu.VMEM((B, 2, 64, N), bf16),
            pltpu.VMEM((4, 4, 64, N), bf16),
            pltpu.VMEM((B, 4, 64, N), bf16),
            pltpu.VMEM((B, 4, 64, N), bf16),
            pltpu.VMEM((4, TOKENS, N), bf16),
            pltpu.VMEM((B, B, N), f32),
            pltpu.VMEM((B, B, N), f32),
            pltpu.VMEM((2, 4, 64, PART), bf16),
            pltpu.VMEM((2, 3, 64, PART), bf16),
            pltpu.VMEM((4, 2, 16, PART), bf16),
            pltpu.VMEM((3, 2, 16, PART), bf16),
            pltpu.VMEM((2, 2, 8, PART), f32),
            dma((8, B)),
            dma((8, B)),
            dma((5, B)),
            dma((5, B)),
            dma((3, B)),
            dma((3, B)),
            dma((4, 4)),
            dma((4, 4)),
            dma((2,)),
            dma((2,)),
            dma((28,)),
            *(pltpu.VMEM((B, *shape), dtype) for shape, dtype in FIELDS.values()),
        ],
        compiler_params=pltpu.CompilerParams(
            collective_id=0, has_side_effects=True, vmem_limit_bytes=56 * 2**20
        ),
    )(doc_lengths, queries, keys, values, directions, beta_logits, out_proj, out_grad)
    dq, dk, dv, du, gp, dl = pl.pallas_call(
        hand_over,
        out_shape=results,
        in_specs=[anywhere] * 6,
        out_specs=[pl.BlockSpec(memory_space=pltpu.VMEM)] * 6,
        scratch_shapes=[dma((6,))],
    )(*made)
    return dq, dk, dv, du, dl, gp


def solution(mesh):
    rows = P("dp", "ctx", None)
    return jax.shard_map(
        per_device,
        mesh=mesh,
        in_specs=(rows, rows, rows, rows, P("dp", None, "ctx"), P(), rows, P("dp", None)),
        out_specs=(rows, rows, rows, rows, P("dp", None, "ctx"), P(("dp", "ctx"), None)),
        check_vma=False,
    )
```

```python
import functools

import jax
import jax.numpy as jnp
from jax import lax
from jax.experimental import pallas as pl
from jax.experimental.pallas import tpu as pltpu
from jax.sharding import PartitionSpec as P

f32, bf16 = jnp.float32, jnp.bfloat16
MESH = pl.DeviceIdType.MESH
N = 128
B = 8
TOKENS = N * B
WIDTH = 4096
PART = WIDTH // 4
HALF = PART // 2
SCALE = N**-0.5
Q, K, U, V, DO = range(5)
FIELDS = {
    "uu": ((N, N), f32), "uk": ((N, N), f32), "inner": ((N, N), f32), "r_row": ((1, N), f32), "r_col": ((N, 1), f32),
    "b_col": ((N, 1), f32), "across": ((N, N), bf16), "inv": ((N, N), bf16), "inv_low": ((N, N), bf16), "yc": ((N, 2 * N), bf16),
    "qhat": ((N, N), bf16), "move": ((N, N), bf16), "ktil": ((N, N), bf16), "d_inner": ((N, N), bf16),
    "d_qbar": ((N, N), f32), "d_ktil": ((N, N), f32), "d_move": ((N, N), bf16),
}
NEAR, NEXT, FAR = (1,), (2, 3, 6, 7), (4, 5)


def dot(a, b, ca, cb):
    return lax.dot_general(
        a.astype(bf16), b.astype(bf16), (((ca,), (cb,)), ((), ())), preferred_element_type=f32
    )


def nn(a, b):
    return dot(a, b, 1, 0)


def nt(a, b):
    return dot(a, b, 1, 1)


def tn(a, b):
    return dot(a, b, 0, 0)


def down(*parts):
    return jnp.concatenate(parts, 0)


def beside(*parts):
    return jnp.concatenate(parts, 1)


def split(x):
    high = x.astype(bf16)
    return high, (x - high.astype(f32)).astype(bf16)


def nn3(a, b):
    ah, al = split(a)
    bh, bl = split(b)
    return nn(beside(ah, al), down(bh, bh)) + nn(ah, bl)


def masks():
    row = lax.broadcasted_iota(jnp.int32, (N, N), 0)
    col = lax.broadcasted_iota(jnp.int32, (N, N), 1)
    return row, col, row == col, row > col, col <= row


def nn3_split(a, b):
    (ah, al), (bh, bl) = a, split(b)
    return nn(beside(ah, al), down(bh, bh)) + nn(ah, bl)


def block_inverse(c, ins, logit, f):
    raw = ins[U, pl.ds(c * N, N)]
    row, col, eye, before, _ = masks()
    uu = nt(raw, raw)
    yield
    diag = jnp.where(eye, uu, 0.0)
    r_row = lax.rsqrt(jnp.sum(diag, 0, keepdims=True) + 1e-6)
    r_col = lax.rsqrt(jnp.sum(diag, 1, keepdims=True) + 1e-6)
    b_row = 2.0 / (1.0 + jnp.exp(-logit))
    b_col = jnp.sum(jnp.where(eye, b_row, 0.0), 1, keepdims=True)
    lower = jnp.where(before, b_col * r_col * uu * r_row, 0.0)
    inv = jnp.where(eye, 1.0, jnp.where((row >> 1) == (col >> 1), -lower, 0.0))
    for level in range(1, 7):
        mask = ((row >> (level + 1)) == (col >> (level + 1))) & ((row >> level) != (col >> level))
        half = nn3(inv, jnp.where(mask, lower, 0.0))
        yield
        inv = inv - nn3(half, inv)
        yield
    f["uu"][c], f["r_row"][c], f["r_col"][c], f["b_col"][c] = uu, r_row, r_col, b_col
    f["inv"][c], f["inv_low"][c] = split(inv)


def block_forward(c, ins, f):
    query, keys, raw = (ins[a, pl.ds(c * N, N)] for a in (Q, K, U))
    _, _, eye, before, within = masks()
    prods = nt(down(raw, query), down(raw, keys))
    yield
    uk, qu, qk = prods[:N, N:], prods[N:, :N], prods[N:, N:]
    r_col = f["r_col"][c]
    br = f["b_col"][c] * r_col
    right = jnp.where(before, br * uk, 0.0)
    across = jnp.where(within, qu * f["r_row"][c], 0.0)
    yc = nn3_split((f["inv"][c], f["inv_low"][c]), beside(br * raw.astype(f32), right))
    yield
    eyc = nn3(across, yc)
    yield
    query_bar = query.astype(f32) - eyc[:, :N]
    inner = qk - eyc[:, N:]
    high, low = split(yc * r_col)
    shift = tn(down(high, low), down(raw, raw))
    yield
    move = jnp.where(eye, 1.0, 0.0) - shift[:N]
    key_tilde = keys.astype(f32) - shift[N:]
    f["uk"][c], f["across"][c], f["yc"][c] = uk, across.astype(bf16), yc.astype(bf16)
    f["qhat"][c], f["move"][c], f["ktil"][c] = query_bar.astype(bf16), move.astype(bf16), key_tilde.astype(bf16)
    f["inner"][c] = inner


def block_backward(c, ins, f):
    query, keys, raw = (ins[a, pl.ds(c * N, N)] for a in (Q, K, U))
    row, col, eye, before, within = masks()
    r_row, r_col, b_col, yc, across = (f[name][c] for name in ("r_row", "r_col", "b_col", "yc", "across"))
    d_in, d_qbar, d_ktil = f["d_inner"][c], f["d_qbar"][c], f["d_ktil"][c]
    w = raw.astype(f32) * r_col
    wb = w.astype(bf16)
    d_qi = beside(d_qbar.astype(bf16), d_in)
    d_mk = down(f["d_move"][c], d_ktil.astype(bf16))
    d_yc = -(tn(across, d_qi) + nt(wb, d_mk))
    yield
    d_across = jnp.where(within, -nt(d_qi, yc), 0.0).astype(bf16)
    yield
    d_br = tn(f["inv"][c], d_yc)
    yield
    d_lower = jnp.where(before, -nt(d_br, yc), 0.0)
    yield
    d_bw, d_right = d_br[:, :N], jnp.where(before, d_br[:, N:], 0.0)
    d_beta = jnp.sum(
        d_right * (r_col * f["uk"][c]) + d_lower * (r_col * f["uu"][c] * r_row) + d_bw * w, 1, keepdims=True
    )
    d_wk = (b_col * d_right).astype(bf16)
    d_gram = (b_col * d_lower).astype(bf16)
    kw, qw = down(keys, wb), down(query, wb)
    d_query = d_qbar + nn(beside(d_in, d_across), kw)
    yield
    d_keys = d_ktil + tn(down(d_in, d_wk), qw)
    yield
    d_w = b_col * d_bw - nn(yc, d_mk) + nn(beside(d_wk, d_gram), kw) + tn(down(d_across, d_gram), qw)
    yield
    d_raw = r_col * (d_w - w * jnp.sum(w * d_w, 1, keepdims=True))
    d_logit = d_beta * b_col * (1.0 - 0.5 * b_col)
    d_logit = jnp.sum(jnp.where(eye, d_logit, 0.0), 0, keepdims=True)
    return d_query.astype(bf16), d_keys.astype(bf16), d_raw.astype(bf16), d_logit


def together(steps):
    steps = list(steps)
    results = [None] * len(steps)
    live = list(range(len(steps)))
    while live:
        for i in list(live):
            try:
                next(steps[i])
            except StopIteration as stop:
                results[i] = stop.value
                live.remove(i)
    return results


def kernel(
    lens, q_in, k_in, v_in, u_in, l_in, proj, grad,
    dq_out, dk_out, dv_out, du_out, gp_out, dl_out,
    ins, logits, grad_own, proj_own, dout_own, grad_z, grad_y, att_own, att, att_z, att_y, made, dl_made, dl_got, prod, rs_first, mid, rs_last,
    in_send, in_recv, out_send, out_recv, att_send, att_recv, rs_send, rs_recv, fin_send, fin_recv, here, *parts,
):
    f = dict(zip(FIELDS, parts))
    dp, me = lax.axis_index("dp"), lax.axis_index("ctx")
    py, pz = lax.div(dp, 4), lax.rem(dp, 4)
    sibling = me + 1 - 2 * lax.rem(me, 2)
    px, core = lax.div(me, 2), lax.rem(me, 2)
    y_at = [lax.rem(py + o, 4) for o in range(4)]
    z_at = [lax.rem(pz + o, 4) for o in range(4)]
    x_at = [lax.rem(px + o, 4) for o in range(4)]
    peers = [x_at[o // 2] * 2 + lax.rem(core + o % 2, 2) for o in range(B)]
    along_y = [(y * 4 + pz, me) for y in y_at]
    along_z = [(py * 4 + z, me) for z in z_at]
    along_x = [(dp, x * 2 + core) for x in x_at]
    z_slot, y_slot = pz * 2 + core, py * 2 + core
    z_group = [(c, (py * 4 + z, px * 2 + c), z) for z in z_at for c in (core, 1 - core)]
    y_group = [(c, (y * 4 + pz, px * 2 + c), y) for y in y_at for c in (core, 1 - core)]
    rows = pl.ds(pl.multiple_of(me * N, N), N)

    def cols(p, width=N):
        return pl.ds(pl.multiple_of(p * width, width), width)

    sent = []

    def send(src, dst, send_sem, recv_sem, device):
        copy = pltpu.make_async_remote_copy(
            src_ref=src, dst_ref=dst, send_sem=send_sem, recv_sem=recv_sem, device_id=device, device_id_type=MESH
        )
        copy.start()
        sent.append(copy)
        return copy

    def local(src, dst, sem):
        copy = pltpu.make_async_copy(src, dst, sem)
        copy.start()
        return copy

    sources = {Q: q_in, K: k_in, U: u_in, V: v_in}
    own = [local(ref.at[0, :, cols(me)], ins.at[a, rows], here.at[a]) for a, ref in sources.items()]
    own.append(local(l_in.at[0], logits.at[me], here.at[4]))
    own_grad = local(grad.at[0], grad_own, here.at[5])
    z_half, y_half = lax.rem(pz, 2), lax.rem(py, 2)
    z_for, y_for = pz - z_half + core, py - y_half + core
    z_rows, y_rows = (pl.ds(pl.multiple_of(slot * N, N), N) for slot in (z_slot, y_slot))
    own_cut = [
        local(grad.at[0, :, cols(z_half, PART)], grad_z.at[z_rows], here.at[6]),
        local(grad.at[0, :, cols(y_half + 2, PART)], grad_y.at[y_rows], here.at[22]),
    ]
    own_proj = [local(proj.at[cols(x_at[dx], 2 * N)], proj_own.at[dx], here.at[8 + dx]) for dx in range(4)]

    barrier = pltpu.get_barrier_semaphore()
    greeted = [(dp, p) for p in peers[1:]] + [d for _, d, _ in y_group[2:] + z_group[2:]]
    z_pair, y_pair = pz + 1 - 2 * z_half, py + 1 - 2 * y_half
    for chip in (py * 4 + z_pair, y_pair * 4 + pz):
        greeted += [(chip, p) for p in peers[2:]]
    for device in greeted:
        pl.semaphore_signal(barrier, inc=1, device_id=device, device_id_type=MESH)
    pl.semaphore_wait(barrier, len(greeted))

    got = {}

    def send_in(a, o):
        if a == 5:
            src, dst = l_in.at[0], logits.at[me]
        else:
            src, dst = sources[a].at[0, :, cols(peers[o])], ins.at[a, rows]
        got[a, o] = send(src, dst, in_send.at[a, o], in_recv.at[a, o], (dp, peers[o]))

    for a in (5, U, K, Q):
        for o in (*NEXT, *FAR, *NEAR):
            send_in(a, o)

    for o in range(1, 4):
        half = lax.rem(z_at[o], 2)
        got[6, o] = send(
            grad.at[0, :, cols(half, PART)], grad_z.at[z_rows], in_send.at[6, o], in_recv.at[6, o], along_z[o]
        )
        half = lax.rem(y_at[o], 2)
        got[7, o] = send(
            grad.at[0, :, cols(half + 2, PART)], grad_y.at[y_rows], in_send.at[7, o], in_recv.at[7, o], along_y[o]
        )
    got[6, 4] = send(
        grad.at[0, :, cols(z_half, PART)], grad_z.at[z_rows], in_send.at[6, 4], in_recv.at[6, 4], (dp, sibling)
    )
    got[7, 4] = send(
        grad.at[0, :, cols(y_half + 2, PART)], grad_y.at[y_rows], in_send.at[7, 4], in_recv.at[7, 4], (dp, sibling)
    )

    for copy in own:
        copy.wait()
    head = lax.broadcasted_iota(jnp.int32, (B, N), 0) == me

    own_grad.wait()
    for dx in (1, 3, 2, 0):
        own_proj[dx].wait()
        both = nt(grad_own[...], proj_own[dx]).astype(bf16)
        for c in range(2):
            dout_own[dx, c] = both[:, c * N : (c + 1) * N]
    own_dout = local(dout_own.at[0, core], ins.at[DO, rows], here.at[7])

    for a in (5, U):
        for o in range(1, B):
            got[a, o].wait_recv()
    own_logits = [jnp.sum(jnp.where(head, logits[c], 0.0), 0, keepdims=True) for c in range(B)]
    for o in (*NEXT, *FAR, *NEAR):
        send_in(V, o)
    for o in (*NEXT, *FAR, *NEAR):
        src = dout_own.at[o // 2, lax.rem(peers[o], 2)]
        got[DO, o] = send(src, ins.at[DO, rows], in_send.at[DO, o], in_recv.at[DO, o], (dp, peers[o]))
    together(block_inverse(c, ins, own_logits[c], f) for c in range(B))
    for a in (K, Q):
        for o in range(1, B):
            got[a, o].wait_recv()
    together(block_forward(c, ins, f) for c in range(B))

    def block(a, c):
        return ins[a, c * N : (c + 1) * N]

    ends = [lens[0, 0]]
    for i in range(1, 4):
        ends.append(ends[-1] + lens[0, i])
    carried, probs = [None] * B, [None] * B

    def carry_on():
        for c in range(1, B):
            new = f["ktil"][c - 1]
            carried[c] = new if c == 1 else down(nn(carried[c - 1], f["move"][c - 1]).astype(bf16), new)
            yield

    def row_forward(c):
        for _ in range(c):
            yield
        span = (c + 1) * N
        place = lax.broadcasted_iota(jnp.int32, (N, 1), 0) + c * N
        start = jnp.zeros((N, 1), jnp.int32)
        for end in ends:
            start = jnp.where(end <= place, jnp.maximum(start, end), start)
        key_place = lax.broadcasted_iota(jnp.int32, (N, span), 1)
        seen = (key_place >= start) & (key_place <= place)
        raw = f["inner"][c] if c == 0 else beside(nt(f["qhat"][c], carried[c]), f["inner"][c])
        yield
        score = jnp.where(seen, raw * SCALE, -1e30)
        peak = jnp.max(score, 1, keepdims=True)
        yield
        part = jnp.exp(score - peak)
        mass = jnp.sum(part, 1, keepdims=True)
        yield
        probs[c] = part * (1.0 / mass)
        yield

    def row_result(c):
        result = nn(probs[c], ins[V, : (c + 1) * N])
        yield
        att_own[c] = result.T.astype(bf16).reshape(2, 64, N)

    together([carry_on(), *(row_forward(c) for c in range(B))])
    for o in range(1, B):
        got[V, o].wait_recv()
    together(row_result(c) for c in range(B))

    own_att = local(att_own.at[me], att.at[lax.div(me, 2), pl.ds(lax.rem(me, 2) * 2, 2)], here.at[23])
    att_got = []
    for o in range(1, B):
        att_got.append(
            send(
                att_own.at[peers[o]], att.at[lax.div(me, 2), pl.ds(lax.rem(me, 2) * 2, 2)],
                att_send.at[0, o], att_recv.at[0, o], (dp, peers[o]),
            )
        )

    for o in range(1, 4):
        for a, at, place in ((6, z_at, grad_z), (7, y_at, grad_y)):
            got[a, o].wait_recv()
            part = place.at[pl.ds(pl.multiple_of((at[4 - o] * 2 + core) * N, N), N)]
            got[a, 4 + o] = send(part, part, in_send.at[a, 4 + o], in_recv.at[a, 4 + o], (dp, sibling))

    own_dout.wait()
    for o in range(1, B):
        got[DO, o].wait_recv()
    d_carried, d_value = [None] * B, [None] * B

    def row_backward(c):
        for _ in range(B - 1 - c):
            yield
        span = (c + 1) * N
        grads, prob = block(DO, c), probs[c]
        d_prob = nt(grads, ins[V, :span])
        yield
        mean = jnp.sum(prob * d_prob, 1, keepdims=True)
        yield
        d_score = prob * (d_prob - mean) * SCALE
        f["d_inner"][c] = d_score[:, c * N :].astype(bf16)
        if c:
            early = d_score[:, : c * N].astype(bf16)
            d_carried[c] = tn(early, f["qhat"][c])
            yield
            f["d_qbar"][c] = nn(early, carried[c])
        else:
            f["d_qbar"][c] = jnp.zeros((N, N), f32)
        yield
        term = tn(prob, grads)
        for j in range(c + 1):
            piece = term[j * N : (j + 1) * N]
            d_value[j] = piece if d_value[j] is None else d_value[j] + piece

    def carry_back():
        f["d_ktil"][B - 1] = jnp.zeros((N, N), f32)
        for c in (0, B - 1):
            f["d_move"][c] = jnp.zeros((N, N), bf16)
        later = None
        for c in range(B - 1, 0, -1):
            while d_carried[c] is None:
                yield
            now = d_carried[c]
            if later is not None:
                back = later[: c * N].astype(bf16)
                now = now + nt(back, f["move"][c])
                f["d_move"][c] = tn(carried[c], back).astype(bf16)
            f["d_ktil"][c - 1] = now[(c - 1) * N :]
            later = now
            yield

    together([*(row_backward(c) for c in range(B - 1, -1, -1)), carry_back()])

    out = {}
    results = (dq_out, dk_out, du_out, dv_out)

    def send_out(i, o):
        src, dst = made.at[i, cols(peers[o])], results[i].at[0, :, cols(me)]
        if o:
            out[i, o] = send(src, dst, out_send.at[i, o], out_recv.at[i, o], (dp, peers[o]))
        else:
            out[i, o] = local(src, dst, here.at[16 + i])

    for j in range(B):
        made[3, j * N : (j + 1) * N] = d_value[j].astype(bf16)
    for o in (*NEXT, *FAR, *NEAR, 0):
        send_out(3, o)

    own_att.wait()
    for copy in att_got:
        copy.wait_recv()
    own_share = [
        local(att.at[:, z_for], att_z.at[z_slot], here.at[24]),
        local(att.at[y_for], att_y.at[y_slot], here.at[25]),
    ]
    shared = []
    for o in range(1, B):
        c, to, z = z_group[o]
        z = z - lax.rem(z, 2) + c
        shared.append(send(att.at[:, z], att_z.at[z_slot], att_send.at[1, o], att_recv.at[1, o], to))
        c, to, y = y_group[o]
        y = y - lax.rem(y, 2) + c
        shared.append(send(att.at[y], att_y.at[y_slot], att_send.at[2, o], att_recv.at[2, o], to))

    for some in (NEXT, FAR + (1, 0)):
        blocks = [peers[o] for o in some]
        for o, c, result in zip(some, blocks, together(block_backward(c, ins, f) for c in blocks)):
            for i in range(3):
                made[i, cols(c)] = result[i]
            dl_made[c] = jnp.where(head, result[3], 0.0)
            for i in range(3):
                send_out(i, o)
            if o:
                out[4, o] = send(dl_made.at[c], dl_got.at[me], out_send.at[4, o], out_recv.at[4, o], (dp, c))
            else:
                out[4, o] = local(dl_made.at[c], dl_got.at[me], here.at[20])

    for copy in own_cut + own_share:
        copy.wait()
    for o in range(4, B):
        got[6, o].wait_recv()
        got[7, o].wait_recv()
    for copy in shared:
        copy.wait_recv()
    att_rows = [beside(*(a[m].reshape(2 * N, N) for m in range(B))) for a in (att_z, att_y)]
    first = {}
    for h in range(2):
        for i, place in enumerate((grad_z, grad_y)):
            prod[i, h] = nn(att_rows[i], place[:, h * HALF : (h + 1) * HALF]).astype(bf16).reshape(4, 64, HALF)
            for o in range(1, 4):
                at, to = (y_at[o], along_y[o]) if i == 0 else (z_at[o], along_z[o])
                first[h, i, o] = send(
                    prod.at[i, h, at], rs_first.at[i, h, o - 1], rs_send.at[2 * i + h, o], rs_recv.at[2 * i + h, o], to
                )
    halves, owners = (z_half, y_half), (py * 4 + z_for, y_for * 4 + pz)

    def last_copy(h, i, dx, c):
        return pltpu.make_async_remote_copy(
            src_ref=mid.at[h, i, x_at[dx], c], dst_ref=rs_last.at[h, i, halves[i], dx],
            send_sem=fin_send.at[4 * h + 2 * i + c, dx], recv_sem=fin_recv.at[4 * h + 2 * i + halves[i], dx],
            device_id=(owners[i], x_at[dx] * 2 + c), device_id_type=MESH,
        )

    def self_copy(h, i, c):
        return pltpu.make_async_copy(mid.at[h, i, px, c], rs_last.at[h, i, halves[i], 0], here.at[26 + 2 * h + i])

    def unless_own(i, c, own_step, step):
        own_one = jnp.logical_and(core == halves[i], core == c)
        pl.when(own_one)(own_step)
        pl.when(jnp.logical_not(own_one))(step)

    for h in range(2):
        for i, own in enumerate((py, pz)):
            for o in range(1, 4):
                first[h, i, o].wait_recv()
            part = prod[i, h, own].astype(f32) + sum(rs_first[i, h, o].astype(f32) for o in range(3))
            for x in range(4):
                for c in range(2):
                    at = (2 * x + c) * 8
                    tile = part[at : at + 8]
                    mid[h, i, x, c] = down(tile[:, : HALF // 2], tile[:, HALF // 2 :]).astype(bf16)
            for dx in (1, 3, 2):
                for c in range(2):
                    last_copy(h, i, dx, c).start()
            for c in range(2):
                unless_own(
                    i, c, functools.partial(lambda *a: self_copy(*a).start(), h, i, c),
                    functools.partial(lambda *a: last_copy(*a).start(), h, i, 0, c),
                )
    for h in range(2):
        for i in range(2):
            for source in range(2):
                for dx in range(4):
                    arrival = pltpu.make_async_remote_copy(
                        src_ref=mid.at[h, i, 0, 0], dst_ref=rs_last.at[h, i, source, dx],
                        send_sem=fin_send.at[4 * h + 2 * i, dx], recv_sem=fin_recv.at[4 * h + 2 * i + source, dx],
                        device_id=(dp, sibling), device_id_type=MESH,
                    )
                    if dx:
                        arrival.wait_recv()
                    else:
                        own_one = jnp.logical_and(core == halves[i], core == source)
                        pl.when(own_one)(functools.partial(lambda *a: self_copy(*a).wait(), h, i, source))
                        pl.when(jnp.logical_not(own_one))(arrival.wait_recv)
                total = sum(rs_last[h, i, source, dx].astype(f32) for dx in range(4))
                at = (2 * i + source) * PART + h * HALF
                gp_out[:, at : at + HALF // 2] = total[:8]
                gp_out[:, at + HALF // 2 : at + HALF] = total[8:]

    for i in range(5):
        out[i, 0].wait()
        for o in range(1, B):
            out[i, o].wait_recv()
    dl_out[0] = sum(dl_got[h] for h in range(B))
    for h in range(2):
        for i in range(2):
            for c in range(2):
                for dx in range(1, 4):
                    last_copy(h, i, dx, c).wait_send()
                unless_own(i, c, lambda: None, functools.partial(lambda *a: last_copy(*a).wait_send(), h, i, 0, c))
    for copy in sent:
        copy.wait_send()


def hand_over(*refs):
    count = (len(refs) - 1) // 2
    sems = refs[-1]
    copies = [pltpu.make_async_copy(refs[i], refs[count + i], sems.at[i]) for i in range(count)]
    for copy in copies:
        copy.start()
    for copy in copies:
        copy.wait()


def per_device(queries, keys, values, directions, beta_logits, out_proj, out_grad, doc_lengths):
    tokens = jax.ShapeDtypeStruct((1, N, TOKENS), bf16)
    anywhere = pl.BlockSpec(memory_space=pl.ANY)
    dma = pltpu.SemaphoreType.DMA
    results = [tokens] * 4 + [jax.ShapeDtypeStruct((B, WIDTH), f32), jax.ShapeDtypeStruct((1, B, N), f32)]
    made = pl.pallas_call(
        kernel,
        out_shape=results,
        in_specs=[pl.BlockSpec(memory_space=pltpu.SMEM)] + [anywhere] * 7,
        out_specs=[anywhere] * 4 + [pl.BlockSpec(memory_space=pltpu.VMEM)] * 2,
        scratch_shapes=[
            pltpu.VMEM((5, TOKENS, N), bf16),
            pltpu.VMEM((B, B, N), f32),
            pltpu.VMEM((N, WIDTH), bf16),
            pltpu.VMEM((4, 2 * N, WIDTH), bf16),
            pltpu.VMEM((4, 2, N, N), bf16),
            pltpu.VMEM((TOKENS, PART), bf16),
            pltpu.VMEM((TOKENS, PART), bf16),
            pltpu.VMEM((B, 2, 64, N), bf16),
            pltpu.VMEM((4, 4, 64, N), bf16),
            pltpu.VMEM((B, 4, 64, N), bf16),
            pltpu.VMEM((B, 4, 64, N), bf16),
            pltpu.VMEM((4, TOKENS, N), bf16),
            pltpu.VMEM((B, B, N), f32),
            pltpu.VMEM((B, B, N), f32),
            pltpu.VMEM((2, 2, 4, 64, HALF), bf16),
            pltpu.VMEM((2, 2, 3, 64, HALF), bf16),
            pltpu.VMEM((2, 2, 4, 2, 16, HALF // 2), bf16),
            pltpu.VMEM((2, 2, 2, 4, 16, HALF // 2), bf16),
            dma((8, B)),
            dma((8, B)),
            dma((5, B)),
            dma((5, B)),
            dma((3, B)),
            dma((3, B)),
            dma((4, 4)),
            dma((4, 4)),
            dma((B, 4)),
            dma((B, 4)),
            dma((30,)),
            *(pltpu.VMEM((B, *shape), dtype) for shape, dtype in FIELDS.values()),
        ],
        compiler_params=pltpu.CompilerParams(
            collective_id=0, has_side_effects=True, vmem_limit_bytes=56 * 2**20
        ),
    )(doc_lengths, queries, keys, values, directions, beta_logits, out_proj, out_grad)
    dq, dk, dv, du, gp, dl = pl.pallas_call(
        hand_over,
        out_shape=results,
        in_specs=[anywhere] * 6,
        out_specs=[pl.BlockSpec(memory_space=pltpu.VMEM)] * 6,
        scratch_shapes=[dma((6,))],
    )(*made)
    return dq, dk, dv, du, dl, gp


def solution(mesh):
    rows = P("dp", "ctx", None)
    return jax.shard_map(
        per_device,
        mesh=mesh,
        in_specs=(rows, rows, rows, rows, P("dp", None, "ctx"), P(), rows, P("dp", None)),
        out_specs=(rows, rows, rows, rows, P("dp", None, "ctx"), P(("dp", "ctx"), None)),
        check_vma=False,
    )
```

```python
import functools

import jax
import jax.numpy as jnp
from jax import lax
from jax.experimental import pallas as pl
from jax.experimental.pallas import tpu as pltpu
from jax.sharding import PartitionSpec as P

f32, bf16 = jnp.float32, jnp.bfloat16
MESH = pl.DeviceIdType.MESH
N = 128
B = 8
TOKENS = N * B
WIDTH = 4096
PART = WIDTH // 4
HALF = PART // 2
SCALE = N**-0.5
Q, K, U, V, DO = range(5)
FIELDS = {
    "uu": ((N, N), f32), "uk": ((N, N), f32), "inner": ((N, N), f32), "r_row": ((1, N), f32), "r_col": ((N, 1), f32),
    "b_col": ((N, 1), f32), "across": ((N, N), bf16), "inv": ((N, N), bf16), "inv_low": ((N, N), bf16), "yc": ((N, 2 * N), bf16),
    "qhat": ((N, N), bf16), "move": ((N, N), bf16), "ktil": ((N, N), bf16), "d_inner": ((N, N), bf16),
    "d_qbar": ((N, N), f32), "d_ktil": ((N, N), f32), "d_move": ((N, N), bf16),
}
NEAR, NEXT, FAR = (1,), (2, 3, 6, 7), (4, 5)


def dot(a, b, ca, cb):
    return lax.dot_general(
        a.astype(bf16), b.astype(bf16), (((ca,), (cb,)), ((), ())), preferred_element_type=f32
    )


def nn(a, b):
    return dot(a, b, 1, 0)


def nt(a, b):
    return dot(a, b, 1, 1)


def tn(a, b):
    return dot(a, b, 0, 0)


def down(*parts):
    return jnp.concatenate(parts, 0)


def beside(*parts):
    return jnp.concatenate(parts, 1)


def split(x):
    high = x.astype(bf16)
    return high, (x - high.astype(f32)).astype(bf16)


def nn3(a, b):
    ah, al = split(a)
    bh, bl = split(b)
    return nn(beside(ah, al), down(bh, bh)) + nn(ah, bl)


def masks():
    row = lax.broadcasted_iota(jnp.int32, (N, N), 0)
    col = lax.broadcasted_iota(jnp.int32, (N, N), 1)
    return row, col, row == col, row > col, col <= row


def nn3_split(a, b):
    (ah, al), (bh, bl) = a, split(b)
    return nn(beside(ah, al), down(bh, bh)) + nn(ah, bl)


def block_inverse(c, ins, logit, f):
    raw = ins[U, pl.ds(c * N, N)]
    row, col, eye, before, _ = masks()
    uu = nt(raw, raw)
    yield
    diag = jnp.where(eye, uu, 0.0)
    r_row = lax.rsqrt(jnp.sum(diag, 0, keepdims=True) + 1e-6)
    r_col = lax.rsqrt(jnp.sum(diag, 1, keepdims=True) + 1e-6)
    b_row = 2.0 / (1.0 + jnp.exp(-logit))
    b_col = jnp.sum(jnp.where(eye, b_row, 0.0), 1, keepdims=True)
    lower = jnp.where(before, b_col * r_col * uu * r_row, 0.0)
    inv = jnp.where(eye, 1.0, jnp.where((row >> 1) == (col >> 1), -lower, 0.0))
    for level in range(1, 7):
        mask = ((row >> (level + 1)) == (col >> (level + 1))) & ((row >> level) != (col >> level))
        half = nn3(inv, jnp.where(mask, lower, 0.0))
        yield
        inv = inv - nn3(half, inv)
        yield
    f["uu"][c], f["r_row"][c], f["r_col"][c], f["b_col"][c] = uu, r_row, r_col, b_col
    f["inv"][c], f["inv_low"][c] = split(inv)


def block_forward(c, ins, f):
    query, keys, raw = (ins[a, pl.ds(c * N, N)] for a in (Q, K, U))
    _, _, eye, before, within = masks()
    prods = nt(down(raw, query), down(raw, keys))
    yield
    uk, qu, qk = prods[:N, N:], prods[N:, :N], prods[N:, N:]
    r_col = f["r_col"][c]
    br = f["b_col"][c] * r_col
    right = jnp.where(before, br * uk, 0.0)
    across = jnp.where(within, qu * f["r_row"][c], 0.0)
    yc = nn3_split((f["inv"][c], f["inv_low"][c]), beside(br * raw.astype(f32), right))
    yield
    eyc = nn3(across, yc)
    yield
    query_bar = query.astype(f32) - eyc[:, :N]
    inner = qk - eyc[:, N:]
    high, low = split(yc * r_col)
    shift = tn(down(high, low), down(raw, raw))
    yield
    move = jnp.where(eye, 1.0, 0.0) - shift[:N]
    key_tilde = keys.astype(f32) - shift[N:]
    f["uk"][c], f["across"][c], f["yc"][c] = uk, across.astype(bf16), yc.astype(bf16)
    f["qhat"][c], f["move"][c], f["ktil"][c] = query_bar.astype(bf16), move.astype(bf16), key_tilde.astype(bf16)
    f["inner"][c] = inner


def block_backward(c, ins, f):
    query, keys, raw = (ins[a, pl.ds(c * N, N)] for a in (Q, K, U))
    row, col, eye, before, within = masks()
    r_row, r_col, b_col, yc, across = (f[name][c] for name in ("r_row", "r_col", "b_col", "yc", "across"))
    d_in, d_qbar, d_ktil = f["d_inner"][c], f["d_qbar"][c], f["d_ktil"][c]
    w = raw.astype(f32) * r_col
    wb = w.astype(bf16)
    d_qi = beside(d_qbar.astype(bf16), d_in)
    d_mk = down(f["d_move"][c], d_ktil.astype(bf16))
    d_yc = -(tn(across, d_qi) + nt(wb, d_mk))
    yield
    d_across = jnp.where(within, -nt(d_qi, yc), 0.0).astype(bf16)
    yield
    high, low = split(d_yc)
    d_br = tn(down(f["inv"][c], f["inv_low"][c]), down(high, high)) + tn(f["inv"][c], low)
    yield
    d_lower = jnp.where(before, -nt(d_br, yc), 0.0)
    yield
    d_bw, d_right = d_br[:, :N], jnp.where(before, d_br[:, N:], 0.0)
    d_beta = jnp.sum(
        d_right * (r_col * f["uk"][c]) + d_lower * (r_col * f["uu"][c] * r_row) + d_bw * w, 1, keepdims=True
    )
    d_wk = (b_col * d_right).astype(bf16)
    d_gram = (b_col * d_lower).astype(bf16)
    kw, qw = down(keys, wb), down(query, wb)
    d_query = d_qbar + nn(beside(d_in, d_across), kw)
    yield
    d_keys = d_ktil + tn(down(d_in, d_wk), qw)
    yield
    d_w = b_col * d_bw - nn(yc, d_mk) + nn(beside(d_wk, d_gram), kw) + tn(down(d_across, d_gram), qw)
    yield
    d_raw = r_col * (d_w - w * jnp.sum(w * d_w, 1, keepdims=True))
    d_logit = d_beta * b_col * (1.0 - 0.5 * b_col)
    d_logit = jnp.sum(jnp.where(eye, d_logit, 0.0), 0, keepdims=True)
    return d_query.astype(bf16), d_keys.astype(bf16), d_raw.astype(bf16), d_logit


def together(steps):
    steps = list(steps)
    results = [None] * len(steps)
    live = list(range(len(steps)))
    while live:
        for i in list(live):
            try:
                next(steps[i])
            except StopIteration as stop:
                results[i] = stop.value
                live.remove(i)
    return results


def kernel(
    lens, q_in, k_in, v_in, u_in, l_in, proj, grad,
    dq_out, dk_out, dv_out, du_out, gp_out, dl_out,
    ins, logits, grad_own, proj_own, dout_own, grad_z, grad_y, att_own, att, att_z, att_y, made, dl_made, dl_got, prod, rs_first, mid, rs_last,
    in_send, in_recv, out_send, out_recv, att_send, att_recv, rs_send, rs_recv, fin_send, fin_recv, here, *parts,
):
    f = dict(zip(FIELDS, parts))
    dp, me = lax.axis_index("dp"), lax.axis_index("ctx")
    py, pz = lax.div(dp, 4), lax.rem(dp, 4)
    sibling = me + 1 - 2 * lax.rem(me, 2)
    px, core = lax.div(me, 2), lax.rem(me, 2)
    y_at = [lax.rem(py + o, 4) for o in range(4)]
    z_at = [lax.rem(pz + o, 4) for o in range(4)]
    x_at = [lax.rem(px + o, 4) for o in range(4)]
    peers = [x_at[o // 2] * 2 + lax.rem(core + o % 2, 2) for o in range(B)]
    along_y = [(y * 4 + pz, me) for y in y_at]
    along_z = [(py * 4 + z, me) for z in z_at]
    along_x = [(dp, x * 2 + core) for x in x_at]
    z_slot, y_slot = pz * 2 + core, py * 2 + core
    z_group = [(c, (py * 4 + z, px * 2 + c), z) for z in z_at for c in (core, 1 - core)]
    y_group = [(c, (y * 4 + pz, px * 2 + c), y) for y in y_at for c in (core, 1 - core)]
    rows = pl.ds(pl.multiple_of(me * N, N), N)

    def cols(p, width=N):
        return pl.ds(pl.multiple_of(p * width, width), width)

    sent = []

    def send(src, dst, send_sem, recv_sem, device):
        copy = pltpu.make_async_remote_copy(
            src_ref=src, dst_ref=dst, send_sem=send_sem, recv_sem=recv_sem, device_id=device, device_id_type=MESH
        )
        copy.start()
        sent.append(copy)
        return copy

    def local(src, dst, sem):
        copy = pltpu.make_async_copy(src, dst, sem)
        copy.start()
        return copy

    sources = {Q: q_in, K: k_in, U: u_in, V: v_in}
    own = [local(ref.at[0, :, cols(me)], ins.at[a, rows], here.at[a]) for a, ref in sources.items()]
    own.append(local(l_in.at[0], logits.at[me], here.at[4]))
    own_grad = local(grad.at[0], grad_own, here.at[5])
    z_half, y_half = lax.rem(pz, 2), lax.rem(py, 2)
    z_for, y_for = pz - z_half + core, py - y_half + core
    z_rows, y_rows = (pl.ds(pl.multiple_of(slot * N, N), N) for slot in (z_slot, y_slot))
    own_cut = [
        local(grad.at[0, :, cols(z_half, PART)], grad_z.at[z_rows], here.at[6]),
        local(grad.at[0, :, cols(y_half + 2, PART)], grad_y.at[y_rows], here.at[22]),
    ]
    own_proj = [local(proj.at[cols(x_at[dx], 2 * N)], proj_own.at[dx], here.at[8 + dx]) for dx in range(4)]

    barrier = pltpu.get_barrier_semaphore()
    greeted = [(dp, p) for p in peers[1:]] + [d for _, d, _ in y_group[2:] + z_group[2:]]
    z_pair, y_pair = pz + 1 - 2 * z_half, py + 1 - 2 * y_half
    for chip in (py * 4 + z_pair, y_pair * 4 + pz):
        greeted += [(chip, p) for p in peers[2:]]
    for device in greeted:
        pl.semaphore_signal(barrier, inc=1, device_id=device, device_id_type=MESH)
    pl.semaphore_wait(barrier, len(greeted))

    got = {}

    def send_in(a, o):
        if a == 5:
            src, dst = l_in.at[0], logits.at[me]
        else:
            src, dst = sources[a].at[0, :, cols(peers[o])], ins.at[a, rows]
        got[a, o] = send(src, dst, in_send.at[a, o], in_recv.at[a, o], (dp, peers[o]))

    for a in (5, U, K, Q):
        for o in (*NEXT, *FAR, *NEAR):
            send_in(a, o)

    for o in range(1, 4):
        half = lax.rem(z_at[o], 2)
        got[6, o] = send(
            grad.at[0, :, cols(half, PART)], grad_z.at[z_rows], in_send.at[6, o], in_recv.at[6, o], along_z[o]
        )
        half = lax.rem(y_at[o], 2)
        got[7, o] = send(
            grad.at[0, :, cols(half + 2, PART)], grad_y.at[y_rows], in_send.at[7, o], in_recv.at[7, o], along_y[o]
        )
    got[6, 4] = send(
        grad.at[0, :, cols(z_half, PART)], grad_z.at[z_rows], in_send.at[6, 4], in_recv.at[6, 4], (dp, sibling)
    )
    got[7, 4] = send(
        grad.at[0, :, cols(y_half + 2, PART)], grad_y.at[y_rows], in_send.at[7, 4], in_recv.at[7, 4], (dp, sibling)
    )

    for copy in own:
        copy.wait()
    head = lax.broadcasted_iota(jnp.int32, (B, N), 0) == me

    own_grad.wait()
    for dx in (1, 3, 2, 0):
        own_proj[dx].wait()
        both = nt(grad_own[...], proj_own[dx]).astype(bf16)
        for c in range(2):
            dout_own[dx, c] = both[:, c * N : (c + 1) * N]
    own_dout = local(dout_own.at[0, core], ins.at[DO, rows], here.at[7])

    for a in (5, U):
        for o in range(1, B):
            got[a, o].wait_recv()
    own_logits = [jnp.sum(jnp.where(head, logits[c], 0.0), 0, keepdims=True) for c in range(B)]
    for o in (*NEXT, *FAR, *NEAR):
        send_in(V, o)
    for o in (*NEXT, *FAR, *NEAR):
        src = dout_own.at[o // 2, lax.rem(peers[o], 2)]
        got[DO, o] = send(src, ins.at[DO, rows], in_send.at[DO, o], in_recv.at[DO, o], (dp, peers[o]))
    together(block_inverse(c, ins, own_logits[c], f) for c in range(B))
    for a in (K, Q):
        for o in range(1, B):
            got[a, o].wait_recv()
    together(block_forward(c, ins, f) for c in range(B))

    def block(a, c):
        return ins[a, c * N : (c + 1) * N]

    ends = [lens[0, 0]]
    for i in range(1, 4):
        ends.append(ends[-1] + lens[0, i])
    carried, probs = [None] * B, [None] * B

    def carry_on():
        for c in range(1, B):
            new = f["ktil"][c - 1]
            carried[c] = new if c == 1 else down(nn(carried[c - 1], f["move"][c - 1]).astype(bf16), new)
            yield

    def row_forward(c):
        for _ in range(c):
            yield
        span = (c + 1) * N
        place = lax.broadcasted_iota(jnp.int32, (N, 1), 0) + c * N
        start = jnp.zeros((N, 1), jnp.int32)
        for end in ends:
            start = jnp.where(end <= place, jnp.maximum(start, end), start)
        key_place = lax.broadcasted_iota(jnp.int32, (N, span), 1)
        seen = (key_place >= start) & (key_place <= place)
        raw = f["inner"][c] if c == 0 else beside(nt(f["qhat"][c], carried[c]), f["inner"][c])
        yield
        score = jnp.where(seen, raw * SCALE, -1e30)
        peak = jnp.max(score, 1, keepdims=True)
        yield
        part = jnp.exp(score - peak)
        mass = jnp.sum(part, 1, keepdims=True)
        yield
        probs[c] = part * (1.0 / mass)
        yield

    def row_result(c):
        result = nn(probs[c], ins[V, : (c + 1) * N])
        yield
        att_own[c] = result.T.astype(bf16).reshape(2, 64, N)

    together([carry_on(), *(row_forward(c) for c in range(B))])
    for o in range(1, B):
        got[V, o].wait_recv()
    together(row_result(c) for c in range(B))

    own_att = local(att_own.at[me], att.at[lax.div(me, 2), pl.ds(lax.rem(me, 2) * 2, 2)], here.at[23])
    att_got = []
    for o in range(1, B):
        att_got.append(
            send(
                att_own.at[peers[o]], att.at[lax.div(me, 2), pl.ds(lax.rem(me, 2) * 2, 2)],
                att_send.at[0, o], att_recv.at[0, o], (dp, peers[o]),
            )
        )

    for o in range(1, 4):
        for a, at, place in ((6, z_at, grad_z), (7, y_at, grad_y)):
            got[a, o].wait_recv()
            part = place.at[pl.ds(pl.multiple_of((at[4 - o] * 2 + core) * N, N), N)]
            got[a, 4 + o] = send(part, part, in_send.at[a, 4 + o], in_recv.at[a, 4 + o], (dp, sibling))

    own_att.wait()
    for copy in att_got:
        copy.wait_recv()
    own_share = [
        local(att.at[:, z_for], att_z.at[z_slot], here.at[24]),
        local(att.at[y_for], att_y.at[y_slot], here.at[25]),
    ]
    shared = []
    for o in range(1, B):
        c, to, z = z_group[o]
        z = z - lax.rem(z, 2) + c
        shared.append(send(att.at[:, z], att_z.at[z_slot], att_send.at[1, o], att_recv.at[1, o], to))
        c, to, y = y_group[o]
        y = y - lax.rem(y, 2) + c
        shared.append(send(att.at[y], att_y.at[y_slot], att_send.at[2, o], att_recv.at[2, o], to))

    own_dout.wait()
    for o in range(1, B):
        got[DO, o].wait_recv()
    d_carried, d_value = [None] * B, [None] * B

    def row_backward(c):
        for _ in range(B - 1 - c):
            yield
        span = (c + 1) * N
        grads, prob = block(DO, c), probs[c]
        d_prob = nt(grads, ins[V, :span])
        yield
        mean = jnp.sum(prob * d_prob, 1, keepdims=True)
        yield
        d_score = prob * (d_prob - mean) * SCALE
        f["d_inner"][c] = d_score[:, c * N :].astype(bf16)
        if c:
            early = d_score[:, : c * N].astype(bf16)
            d_carried[c] = tn(early, f["qhat"][c])
            yield
            f["d_qbar"][c] = nn(early, carried[c])
        else:
            f["d_qbar"][c] = jnp.zeros((N, N), f32)
        yield
        term = tn(prob, grads)
        for j in range(c + 1):
            piece = term[j * N : (j + 1) * N]
            d_value[j] = piece if d_value[j] is None else d_value[j] + piece

    def carry_back():
        f["d_ktil"][B - 1] = jnp.zeros((N, N), f32)
        for c in (0, B - 1):
            f["d_move"][c] = jnp.zeros((N, N), bf16)
        later = None
        for c in range(B - 1, 0, -1):
            while d_carried[c] is None:
                yield
            now = d_carried[c]
            if later is not None:
                back = later[: c * N].astype(bf16)
                now = now + nt(back, f["move"][c])
                f["d_move"][c] = tn(carried[c], back).astype(bf16)
            f["d_ktil"][c - 1] = now[(c - 1) * N :]
            later = now
            yield

    together([*(row_backward(c) for c in range(B - 1, -1, -1)), carry_back()])

    out = {}
    results = (dq_out, dk_out, du_out, dv_out)

    def send_out(i, o):
        src, dst = made.at[i, cols(peers[o])], results[i].at[0, :, cols(me)]
        if o:
            out[i, o] = send(src, dst, out_send.at[i, o], out_recv.at[i, o], (dp, peers[o]))
        else:
            out[i, o] = local(src, dst, here.at[16 + i])

    for j in range(B):
        made[3, j * N : (j + 1) * N] = d_value[j].astype(bf16)
    for o in (*NEXT, *FAR, *NEAR, 0):
        send_out(3, o)

    for some in (NEXT, FAR + (1, 0)):
        blocks = [peers[o] for o in some]
        for o, c, result in zip(some, blocks, together(block_backward(c, ins, f) for c in blocks)):
            for i in range(3):
                made[i, cols(c)] = result[i]
            dl_made[c] = jnp.where(head, result[3], 0.0)
            for i in range(3):
                send_out(i, o)
            if o:
                out[4, o] = send(dl_made.at[c], dl_got.at[me], out_send.at[4, o], out_recv.at[4, o], (dp, c))
            else:
                out[4, o] = local(dl_made.at[c], dl_got.at[me], here.at[20])

    for copy in own_cut + own_share:
        copy.wait()
    for o in range(4, B):
        got[6, o].wait_recv()
        got[7, o].wait_recv()
    for copy in shared:
        copy.wait_recv()
    att_rows = [beside(*(a[m].reshape(2 * N, N) for m in range(B))) for a in (att_z, att_y)]
    first = {}
    for h in range(2):
        for i, place in enumerate((grad_z, grad_y)):
            prod[i, h] = nn(att_rows[i], place[:, h * HALF : (h + 1) * HALF]).astype(bf16).reshape(4, 64, HALF)
            for o in range(1, 4):
                at, to = (y_at[o], along_y[o]) if i == 0 else (z_at[o], along_z[o])
                first[h, i, o] = send(
                    prod.at[i, h, at], rs_first.at[i, h, o - 1], rs_send.at[2 * i + h, o], rs_recv.at[2 * i + h, o], to
                )
    halves, owners = (z_half, y_half), (py * 4 + z_for, y_for * 4 + pz)

    def last_copy(h, i, dx, c):
        return pltpu.make_async_remote_copy(
            src_ref=mid.at[h, i, x_at[dx], c], dst_ref=rs_last.at[h, i, halves[i], dx],
            send_sem=fin_send.at[4 * h + 2 * i + c, dx], recv_sem=fin_recv.at[4 * h + 2 * i + halves[i], dx],
            device_id=(owners[i], x_at[dx] * 2 + c), device_id_type=MESH,
        )

    def self_copy(h, i, c):
        return pltpu.make_async_copy(mid.at[h, i, px, c], rs_last.at[h, i, halves[i], 0], here.at[26 + 2 * h + i])

    def unless_own(i, c, own_step, step):
        own_one = jnp.logical_and(core == halves[i], core == c)
        pl.when(own_one)(own_step)
        pl.when(jnp.logical_not(own_one))(step)

    for h in range(2):
        for i, own in enumerate((py, pz)):
            for o in range(1, 4):
                first[h, i, o].wait_recv()
            part = prod[i, h, own].astype(f32) + sum(rs_first[i, h, o].astype(f32) for o in range(3))
            for x in range(4):
                for c in range(2):
                    at = (2 * x + c) * 8
                    tile = part[at : at + 8]
                    mid[h, i, x, c] = down(tile[:, : HALF // 2], tile[:, HALF // 2 :]).astype(bf16)
            for dx in (1, 3, 2):
                for c in range(2):
                    last_copy(h, i, dx, c).start()
            for c in range(2):
                unless_own(
                    i, c, functools.partial(lambda *a: self_copy(*a).start(), h, i, c),
                    functools.partial(lambda *a: last_copy(*a).start(), h, i, 0, c),
                )
    for h in range(2):
        for i in range(2):
            for source in range(2):
                for dx in range(4):
                    arrival = pltpu.make_async_remote_copy(
                        src_ref=mid.at[h, i, 0, 0], dst_ref=rs_last.at[h, i, source, dx],
                        send_sem=fin_send.at[4 * h + 2 * i, dx], recv_sem=fin_recv.at[4 * h + 2 * i + source, dx],
                        device_id=(dp, sibling), device_id_type=MESH,
                    )
                    if dx:
                        arrival.wait_recv()
                    else:
                        own_one = jnp.logical_and(core == halves[i], core == source)
                        pl.when(own_one)(functools.partial(lambda *a: self_copy(*a).wait(), h, i, source))
                        pl.when(jnp.logical_not(own_one))(arrival.wait_recv)
                total = sum(rs_last[h, i, source, dx].astype(f32) for dx in range(4))
                at = (2 * i + source) * PART + h * HALF
                gp_out[:, at : at + HALF // 2] = total[:8]
                gp_out[:, at + HALF // 2 : at + HALF] = total[8:]

    for i in range(5):
        out[i, 0].wait()
        for o in range(1, B):
            out[i, o].wait_recv()
    dl_out[0] = sum(dl_got[h] for h in range(B))
    for h in range(2):
        for i in range(2):
            for c in range(2):
                for dx in range(1, 4):
                    last_copy(h, i, dx, c).wait_send()
                unless_own(i, c, lambda: None, functools.partial(lambda *a: last_copy(*a).wait_send(), h, i, 0, c))
    for copy in sent:
        copy.wait_send()


def hand_over(*refs):
    count = (len(refs) - 1) // 2
    sems = refs[-1]
    copies = [pltpu.make_async_copy(refs[i], refs[count + i], sems.at[i]) for i in range(count)]
    for copy in copies:
        copy.start()
    for copy in copies:
        copy.wait()


def per_device(queries, keys, values, directions, beta_logits, out_proj, out_grad, doc_lengths):
    tokens = jax.ShapeDtypeStruct((1, N, TOKENS), bf16)
    anywhere = pl.BlockSpec(memory_space=pl.ANY)
    dma = pltpu.SemaphoreType.DMA
    results = [tokens] * 4 + [jax.ShapeDtypeStruct((B, WIDTH), f32), jax.ShapeDtypeStruct((1, B, N), f32)]
    made = pl.pallas_call(
        kernel,
        out_shape=results,
        in_specs=[pl.BlockSpec(memory_space=pltpu.SMEM)] + [anywhere] * 7,
        out_specs=[anywhere] * 4 + [pl.BlockSpec(memory_space=pltpu.VMEM)] * 2,
        scratch_shapes=[
            pltpu.VMEM((5, TOKENS, N), bf16),
            pltpu.VMEM((B, B, N), f32),
            pltpu.VMEM((N, WIDTH), bf16),
            pltpu.VMEM((4, 2 * N, WIDTH), bf16),
            pltpu.VMEM((4, 2, N, N), bf16),
            pltpu.VMEM((TOKENS, PART), bf16),
            pltpu.VMEM((TOKENS, PART), bf16),
            pltpu.VMEM((B, 2, 64, N), bf16),
            pltpu.VMEM((4, 4, 64, N), bf16),
            pltpu.VMEM((B, 4, 64, N), bf16),
            pltpu.VMEM((B, 4, 64, N), bf16),
            pltpu.VMEM((4, TOKENS, N), bf16),
            pltpu.VMEM((B, B, N), f32),
            pltpu.VMEM((B, B, N), f32),
            pltpu.VMEM((2, 2, 4, 64, HALF), bf16),
            pltpu.VMEM((2, 2, 3, 64, HALF), bf16),
            pltpu.VMEM((2, 2, 4, 2, 16, HALF // 2), bf16),
            pltpu.VMEM((2, 2, 2, 4, 16, HALF // 2), bf16),
            dma((8, B)),
            dma((8, B)),
            dma((5, B)),
            dma((5, B)),
            dma((3, B)),
            dma((3, B)),
            dma((4, 4)),
            dma((4, 4)),
            dma((B, 4)),
            dma((B, 4)),
            dma((30,)),
            *(pltpu.VMEM((B, *shape), dtype) for shape, dtype in FIELDS.values()),
        ],
        compiler_params=pltpu.CompilerParams(
            collective_id=0, has_side_effects=True, vmem_limit_bytes=56 * 2**20
        ),
    )(doc_lengths, queries, keys, values, directions, beta_logits, out_proj, out_grad)
    dq, dk, dv, du, gp, dl = pl.pallas_call(
        hand_over,
        out_shape=results,
        in_specs=[anywhere] * 6,
        out_specs=[pl.BlockSpec(memory_space=pltpu.VMEM)] * 6,
        scratch_shapes=[dma((6,))],
    )(*made)
    return dq, dk, dv, du, dl, gp


def solution(mesh):
    rows = P("dp", "ctx", None)
    return jax.shard_map(
        per_device,
        mesh=mesh,
        in_specs=(rows, rows, rows, rows, P("dp", None, "ctx"), P(), rows, P("dp", None)),
        out_specs=(rows, rows, rows, rows, P("dp", None, "ctx"), P(("dp", "ctx"), None)),
        check_vma=False,
    )
```
